256 devices in a mesh: uly: 4 (over x), inner: 16 (over y, z_lo), outer: 4 (over z_hi, core).
Axes of the slice: x: 4, y: 4, z: 8 (z_hi: 2, z_lo: 4; z = z_hi * 4 + z_lo), core: 2. Of those that a mesh axis runs over, the one named last changes fastest.
Arguments:
- query: bfloat16 [32768, 8192], P(('uly', 'inner', 'outer')), may hold values from -6 to 6
- key_proj: bfloat16 [32768, 512], P(('uly', 'inner', 'outer')), may hold values from -5 to 5
- value_projection: bfloat16 [32768, 512], P(('uly', 'inner', 'outer')), may hold values from -6 to 6
- upstream: bfloat16 [32768, 8192], P(('uly', 'inner', 'outer')), may hold values from -6 to 6
- doc_start: int32 [4, 8192], P(None, ('inner', 'outer')), may hold values from 0 to 32767
Outputs:
- attn_out: bfloat16 [32768, 8192], P(('uly', 'inner', 'outer'))
- grad_query: bfloat16 [32768, 8192], P(('uly', 'inner', 'outer'))
- grad_key: bfloat16 [32768, 512], P(('uly', 'inner', 'outer'))
- grad_value: bfloat16 [32768, 512], P(('uly', 'inner', 'outer'))
The draws below stay inside these ranges and needn't reach their ends.
All inputs are finite; a program needn't handle non-finite values.
Results may differ from the reference program's by a relative error of at most 0.035.
Values may be sent and summed in bfloat16 or wider, within the bound.
A program may use at most 128 MiB of HBM per device.

```python
import jax
import jax.numpy as jnp
from jax import lax

QUERY_HEAD_COUNT = 64
KEY_VALUE_HEADS = 4
HEAD_DIMENSION = 128
TOK_DEV = 128
BLOCKS = 64
SPAN = 256
TOKEN_COUNT = 32768
N_ULY = 4


def row_positions():
    place = jnp.arange(TOKEN_COUNT, dtype=jnp.int32)
    row_u = place // (BLOCKS * TOK_DEV)
    row_b = place // TOK_DEV % BLOCKS
    row_w = row_u * TOK_DEV + place % TOK_DEV
    row_span = jnp.where(row_w >= SPAN, 2 * BLOCKS - 1 - row_b, row_b)
    return (row_span * SPAN + row_w % SPAN).astype(jnp.int32)


def draw_query(key, part):
    key = jax.random.fold_in(key, 21)
    value_entries = jnp.clip(jax.random.normal(key, (TOKEN_COUNT, QUERY_HEAD_COUNT * HEAD_DIMENSION), jnp.float32), -5.0, 5.0)
    return value_entries.astype(jnp.bfloat16)


def draw_key_proj(key, part):
    key = jax.random.fold_in(key, 22)
    value_entries = jnp.clip(jax.random.normal(key, (TOKEN_COUNT, KEY_VALUE_HEADS * HEAD_DIMENSION), jnp.float32), -5.0, 5.0)
    return value_entries.astype(jnp.bfloat16)


def draw_doc_start(key, part):
    key = jax.random.fold_in(key, 31)
    place = jnp.arange(TOKEN_COUNT, dtype=jnp.int32)
    opens = jnp.logical_or(jax.random.randint(key, (TOKEN_COUNT,), 0, 2 * SPAN) == 0, place == 0)
    opens = jnp.logical_or(opens, place == TOKEN_COUNT - 1)
    natural = lax.cummax(jnp.where(opens, place, 0), axis=0)
    return natural[row_positions()].reshape(N_ULY, BLOCKS * TOK_DEV)


def steps_of(key, extent, cuts, least, largest):
    def one(axis_at, parts):
        heights = jax.random.uniform(jax.random.fold_in(jax.random.fold_in(key, 6), axis_at), (parts,), jnp.float32, least / len(cuts), largest / len(cuts))
        return jnp.repeat(jnp.exp(heights), extent[axis_at] // parts).reshape((-1,) + (1,) * (len(extent) - axis_at - 1))

    level = one(*cuts[0])
    for cut in cuts[1:]:
        level = level * one(*cut)
    return level


def noise(rng, extent, scale, reach, pieces=(), held_as=jnp.bfloat16):
    level = steps_of(rng, extent, pieces, -0.22, 0.18) if pieces else 1.0
    values = jax.random.normal(rng, extent, jnp.float32) * scale * level
    return jnp.minimum(jnp.maximum(values, -reach), reach).astype(held_as)


def setup_inputs(seed: int = 0) -> dict:
    seeds = jax.random.split(jax.random.key(seed), 6)
    return {
        "query": draw_query(jax.random.fold_in(seeds[5], 71), 0),
        "key_proj": draw_key_proj(jax.random.fold_in(seeds[5], 71), 0),
        "value_projection": noise(seeds[2], (TOKEN_COUNT, KEY_VALUE_HEADS * HEAD_DIMENSION), 1.0, 6.0, ((0, 256),)),
        "upstream": noise(seeds[3], (TOKEN_COUNT, QUERY_HEAD_COUNT * HEAD_DIMENSION), 1.0, 6.0, ((0, 256),)),
        "doc_start": draw_doc_start(jax.random.fold_in(seeds[5], 71), 0),
    }


def attend_head(queries, upstream, query_pos, query_start, keys, value_entries, key_pos, key_live, window):
    row_count = queries.shape[0]
    head_size = keys.shape[1]
    group_size = queries.shape[1] // head_size
    score_scale = head_size ** -0.5
    query_heads = queries.reshape(row_count, group_size, head_size).astype(jnp.float32)
    upstream_heads = upstream.reshape(row_count, group_size, head_size).astype(jnp.float32)
    keys_wide = keys.astype(jnp.float32)
    values_wide = value_entries.astype(jnp.float32)
    allowed = (key_pos[None, :] <= query_pos[:, None]) & (key_pos[None, :] >= query_start[:, None])
    allowed = allowed & (query_pos[:, None] - key_pos[None, :] < window) & key_live[None, :]
    scores = jnp.einsum("rgd,kd->grk", query_heads, keys_wide) * score_scale
    scores = jnp.where(allowed[None], scores, -jnp.inf)
    row_max = jnp.max(scores, axis=2, keepdims=True)
    log_total = row_max + jnp.log(jnp.sum(jnp.exp(scores - row_max), axis=2, keepdims=True))
    weights = jnp.exp(scores - log_total)
    rounded = weights.astype(jnp.bfloat16)
    attn_rows = jnp.einsum("grk,kd->rgd", rounded.astype(jnp.float32), values_wide).astype(jnp.bfloat16)
    row_delta = jnp.einsum("rgd,rgd->gr", upstream_heads, attn_rows.astype(jnp.float32))
    grad_probs = jnp.einsum("rgd,kd->grk", upstream_heads, values_wide)
    pushed = (weights * (grad_probs - row_delta[:, :, None]) * score_scale).astype(jnp.bfloat16)
    pushed_wide = pushed.astype(jnp.float32)
    grad_query = jnp.einsum("grk,kd->rgd", pushed_wide, keys_wide).astype(jnp.bfloat16)
    grad_key = jnp.einsum("grk,rgd->kd", pushed_wide, query_heads)
    grad_value = jnp.einsum("grk,rgd->kd", rounded.astype(jnp.float32), upstream_heads)
    return attn_rows.reshape(row_count, -1), grad_query.reshape(row_count, -1), grad_key, grad_value


def attend_set(queries, upstream, query_pos, query_start, keys, value_entries, key_pos, key_live, window):
    kv_count = keys.shape[1] // HEAD_DIMENSION
    q_width = queries.shape[1] // kv_count
    results = []
    for kv_head in range(kv_count):
        q_cols = slice(kv_head * q_width, (kv_head + 1) * q_width)
        k_cols = slice(kv_head * HEAD_DIMENSION, (kv_head + 1) * HEAD_DIMENSION)
        results.append(attend_head(queries[:, q_cols], upstream[:, q_cols], query_pos, query_start,
                                   keys[:, k_cols], value_entries[:, k_cols], key_pos, key_live, window))
    return tuple(jnp.concatenate([result_row[part_id] for result_row in results], axis=1) for part_id in range(4))


def reference(query, key_proj, value_projection, upstream, doc_start):
    place = jnp.arange(TOKEN_COUNT, dtype=jnp.int32)
    span_id = place // SPAN
    offset = place % SPAN
    second = span_id >= BLOCKS
    block_id = jnp.where(second, 2 * BLOCKS - 1 - span_id, span_id)
    within = second.astype(jnp.int32) * SPAN + offset
    source_row = (within // TOK_DEV) * (BLOCKS * TOK_DEV) + block_id * TOK_DEV + within % TOK_DEV
    row_u = place // (BLOCKS * TOK_DEV)
    row_b = (place // TOK_DEV) % BLOCKS
    row_w = row_u * TOK_DEV + place % TOK_DEV
    row_span = jnp.where(row_w >= SPAN, 2 * BLOCKS - 1 - row_b, row_b)
    row_position = (row_span * SPAN + row_w % SPAN).astype(jnp.int32)

    count = 2 * BLOCKS
    q_nat = query[source_row].reshape(count, SPAN, -1)
    up_nat = upstream[source_row].reshape(count, SPAN, -1)
    k_nat = key_proj[source_row].reshape(count, SPAN, -1)
    v_nat = value_projection[source_row].reshape(count, SPAN, -1)
    start_nat = doc_start.reshape(-1)[source_row].reshape(count, SPAN)
    pos_nat = place.reshape(count, SPAN)
    k_prev = jnp.concatenate((jnp.zeros_like(k_nat[:1]), k_nat[:-1]), axis=0)
    v_prev = jnp.concatenate((jnp.zeros_like(v_nat[:1]), v_nat[:-1]), axis=0)
    index_nat = jnp.arange(count, dtype=jnp.int32)

    def one_span(packed):
        q_rows, up_rows, k_old, v_old, k_new, v_new, pos_rows, start_rows, span_index = packed
        keys = jnp.concatenate((k_old, k_new), axis=0)
        value_entries = jnp.concatenate((v_old, v_new), axis=0)
        key_pos = jnp.concatenate((pos_rows - SPAN, pos_rows))
        key_live = jnp.concatenate((jnp.broadcast_to(span_index > 0, (SPAN,)), jnp.ones((SPAN,), bool)))
        attn_rows, grad_q, grad_k, grad_v = attend_set(q_rows, up_rows, pos_rows, start_rows, keys, value_entries,
                                                       key_pos, key_live, SPAN)
        return attn_rows, grad_q, grad_k[:SPAN], grad_k[SPAN:], grad_v[:SPAN], grad_v[SPAN:]

    attn_c, gq_c, gk_old, gk_new, gv_old, gv_new = lax.map(
        one_span, (q_nat, up_nat, k_prev, v_prev, k_nat, v_nat, pos_nat, start_nat, index_nat))
    gk_total = gk_new + jnp.concatenate((gk_old[1:], jnp.zeros_like(gk_old[:1])), axis=0)
    gv_total = gv_new + jnp.concatenate((gv_old[1:], jnp.zeros_like(gv_old[:1])), axis=0)
    attn_out = attn_c.reshape(TOKEN_COUNT, -1)[row_position]
    grad_query = gq_c.reshape(TOKEN_COUNT, -1)[row_position]
    grad_key = gk_total.reshape(TOKEN_COUNT, -1).astype(jnp.bfloat16)[row_position]
    grad_value = gv_total.reshape(TOKEN_COUNT, -1).astype(jnp.bfloat16)[row_position]
    return attn_out, grad_query, grad_key, grad_value
```

```python
import functools
import math

import jax
import jax.numpy as jnp
from jax import lax
from jax.experimental import pallas as pl
from jax.experimental.pallas import tpu as pltpu
from jax.sharding import PartitionSpec as P

MESH = pl.DeviceIdType.MESH
D = 128
T = 128
HEADS = 4
R = HEADS * T
S = 3 * T
ROWS = 128
MASKED = -1e30

NN = (((1,), (0,)), ((), ()))


def dot(a, b):
    return lax.dot_general(a, b, NN, preferred_element_type=jnp.float32)


def kernel(
    mesh_shape, groups, heads,
    q_hbm, k_hbm, v_hbm, up_hbm, st_hbm,
    o_vm, gq_vm, gk_vm, gv_vm,
    q_vm, up_vm, st_vm, kv, fan_in, fan_out, tri, bias,
    s_0, s_1, w_0, w_1,
    acc, own, old, xsnd, xrcv, zsnd, zrcv,
    load_sem, st_sem, own_sem, prev_send, prev_recv, old_send, old_recv,
    gx_send, gx_recv, gz_send, gz_recv,
):
    n_inner, n_outer = mesh_shape
    blocks = n_inner * n_outer
    chunks = 4 * blocks
    width = heads * D
    per_group = heads // HEADS
    stages = groups * per_group
    steps = per_group // 2
    scale = D ** -0.5
    rate = scale * math.log2(math.e)

    u = lax.axis_index("uly")
    b = lax.axis_index("inner") * n_outer + lax.axis_index("outer")
    late = u // 2
    half = u - 2 * late
    span = b + late * (2 * blocks - 1 - 2 * b)
    chunk = 2 * span + half
    odd = half == 1

    def device_of(c):
        s = c // 2
        is_late = s // blocks
        blk = s + is_late * (2 * blocks - 1 - 2 * s)
        return (c - 2 * s + 2 * is_late, blk // n_outer, blk % n_outer)

    partner = (u + 1 - 2 * half, lax.axis_index("inner"), lax.axis_index("outer"))
    after = device_of((chunk + 2) % chunks)
    before = device_of((chunk + chunks - 2) % chunks)

    def cols(g):
        return pl.ds(pl.multiple_of(g * width, width), width)

    def load(g):
        return (
            pltpu.make_async_copy(q_hbm.at[:, cols(g)], q_vm.at[g], load_sem.at[g, 0]),
            pltpu.make_async_copy(up_hbm.at[:, cols(g)], up_vm.at[g], load_sem.at[g, 1]),
        )

    def load_own(g):
        return tuple(
            pltpu.make_async_copy(
                src.at[:, pl.ds(g * D, D)], kv.at[g, i, pl.ds(0, T)], own_sem.at[g, i])
            for i, src in enumerate((k_hbm, v_hbm))
        )

    def send_old(g):
        return pltpu.make_async_remote_copy(
            src_ref=kv.at[g, :, pl.ds(0, T)], dst_ref=kv.at[g, :, pl.ds(2 * T, T)],
            send_sem=old_send.at[g], recv_sem=old_recv.at[g],
            device_id=after, device_id_type=MESH)

    def send_prev(g):
        return pltpu.make_async_remote_copy(
            src_ref=kv.at[g, :, pl.ds(pl.multiple_of(half * (2 * T), T), T)],
            dst_ref=kv.at[g, :, pl.ds(T, T)],
            send_sem=prev_send.at[g], recv_sem=prev_recv.at[g],
            device_id=partner, device_id_type=MESH)

    def grad_x(g):
        return pltpu.make_async_remote_copy(
            src_ref=xsnd.at[g], dst_ref=xrcv.at[g], send_sem=gx_send.at[g],
            recv_sem=gx_recv.at[g], device_id=partner, device_id_type=MESH)

    def grad_z(g):
        return pltpu.make_async_remote_copy(
            src_ref=zsnd.at[g], dst_ref=zrcv.at[g], send_sem=gz_send.at[g],
            recv_sem=gz_recv.at[g], device_id=before, device_id_type=MESH)

    barrier = pltpu.get_barrier_semaphore()
    for peer in (partner, after, before):
        pl.semaphore_signal(barrier, inc=1, device_id=peer, device_id_type=MESH)

    starts = pltpu.make_async_copy(st_hbm, st_vm, st_sem)
    for g in range(groups):
        for copy in load_own(g):
            copy.start()
    starts.start()
    for g in range(groups):
        for copy in load(g):
            copy.start()

    for copy in load_own(0):
        copy.wait()
    pl.semaphore_wait(barrier, 3)
    send_old(0).start()

    @pl.when(jnp.logical_not(odd))
    def _():
        send_prev(0).start()

    for g in range(1, groups):
        for copy in load_own(g):
            copy.wait()

    starts.wait()
    first = st_vm[0:1, :]
    for i in range(1, 4):
        first = jnp.where(u == i, st_vm[i : i + 1, :], first)
    first = first - chunk * T
    key_at = lax.broadcasted_iota(jnp.int32, (T, T), 0)
    query_at = lax.broadcasted_iota(jnp.int32, (T, T), 1)
    seen = (
        (key_at <= query_at) & (key_at >= first),
        key_at - T >= first,
        (key_at > query_at) & (key_at - 2 * T >= first),
    )
    near = jnp.where(seen[0] | seen[2], 0.0, MASKED)
    bias[:, :T] = near.T
    bias[:, T:] = jnp.where(seen[1], 0.0, MASKED).T
    tri[...] = jnp.where(key_at >= query_at, 1.0, 0.0).astype(jnp.bfloat16)
    fan_in[...] = jnp.zeros_like(fan_in)
    fan_out[...] = jnp.zeros_like(fan_out)

    send_old(0).wait_send()
    send_old(1).start()

    @pl.when(jnp.logical_not(odd))
    def _():
        for g in range(1, groups):
            send_prev(g).start()

    def forward_old(g):
        send_old(g).wait_recv()
        send_prev(g).start()

    @pl.when(odd)
    def _():
        forward_old(0)

    def begin_group(g):
        @pl.when(jnp.logical_not(odd))
        def _():
            send_old(g).wait_recv()

        send_prev(g).wait_recv()
        for copy in load(g):
            copy.wait()
        fan_in[g, :D, :S] = kv[g, 0].T
        fan_in[g, D:, S:] = kv[g, 1].T
        fan_out[g, :S, :D] = kv[g, 1]
        fan_out[g, S:, D:] = kv[g, 0]

    def lanes_of(n):
        at = (n % per_group) * R
        return [pl.ds(pl.multiple_of(at + i * D, D), D) for i in range(HEADS)]

    def rows_of(ref, n):
        return jnp.concatenate([ref[n // per_group, :, c] for c in lanes_of(n)], axis=0)

    def scores(n, s_out):
        n = jnp.minimum(n, stages - 1)
        both = jnp.concatenate([rows_of(q_vm, n), rows_of(up_vm, n)], axis=1)
        s_out[...] = dot(both, fan_in[n // per_group])

    def soften(s_ref, w_out):
        for at in range(0, R, ROWS):
            rows = slice(at, at + ROWS)
            own_k, mid_k, old_k = [slice(i * T, (i + 1) * T) for i in range(3)]
            own_v, mid_v, old_v = [slice(i * T, (i + 1) * T) for i in range(3, 6)]
            here = slice(at % T, at % T + ROWS)
            key_at = lax.broadcasted_iota(jnp.int32, (ROWS, T), 1)
            query_at = lax.broadcasted_iota(jnp.int32, (ROWS, T), 0) + at % T
            lower = key_at <= query_at
            s_mix = jnp.where(lower, s_ref[rows, own_k], s_ref[rows, old_k]) + bias[here, :T]
            s_mid = s_ref[rows, mid_k] + bias[here, T:]
            top = jnp.max(jnp.maximum(s_mix, s_mid), axis=1, keepdims=True)
            e_mix = jnp.exp2((s_mix - top) * rate)
            e_mid = jnp.exp2((s_mid - top) * rate)
            inverse = 1.0 / jnp.sum(e_mix + e_mid, axis=1, keepdims=True)
            dp_mix = jnp.where(lower, s_ref[rows, own_v], s_ref[rows, old_v])
            dp_mid = s_ref[rows, mid_v]
            w_mix = e_mix * inverse
            w_mid = e_mid * inverse
            delta = jnp.sum(w_mix * dp_mix + w_mid * dp_mid, axis=1, keepdims=True)
            ds_mix = w_mix * (dp_mix - delta)
            ds_mid = w_mid * (dp_mid - delta)
            for mix, mid, base in ((w_mix, w_mid, 0), (ds_mix, ds_mid, S)):
                mix = mix.astype(jnp.bfloat16)
                own_part = mix * tri[here, :]
                w_out[rows, base : base + T] = own_part
                w_out[rows, base + T : base + 2 * T] = mid.astype(jnp.bfloat16)
                w_out[rows, base + 2 * T : base + S] = mix - own_part

    def results(n, w_ref):
        n = jnp.maximum(n, 0)
        both = dot(w_ref[...], fan_out[n // per_group])
        acc[1] += dot(rows_of(up_vm, n).T, w_ref[:, :S])
        acc[0] += dot(rows_of(q_vm, n).T, w_ref[:, S:])
        for i in range(HEADS):
            lanes = pl.ds(pl.multiple_of(n * R + i * D, D), D)
            rows = slice(i * T, (i + 1) * T)
            o_vm[:, lanes] = both[rows, :D].astype(jnp.bfloat16)
            gq_vm[:, lanes] = (both[rows, D:] * scale).astype(jnp.bfloat16)

    def finish_group(g):
        for i in range(2):
            grad = acc[i] * scale if i == 0 else acc[i]
            own[g, i] = grad[:, :T].T
            xsnd[g, i] = grad[:, T : 2 * T].T.astype(jnp.bfloat16)
            old[g, i] = grad[:, 2 * T :].T
        acc[...] = jnp.zeros_like(acc)
        grad_x(g).start()

        @pl.when(jnp.logical_not(odd))
        def _():
            zsnd[g] = old[g].astype(jnp.bfloat16)
            grad_z(g).start()

    def pass_back(g):
        @pl.when(odd)
        def _():
            grad_x(g).wait_recv()
            zsnd[g] = (old[g] + xrcv[g].astype(jnp.float32)).astype(jnp.bfloat16)
            grad_z(g).start()

    begin_group(0)
    acc[...] = jnp.zeros_like(acc)
    w_1[...] = jnp.zeros_like(w_1)
    scores(0, s_0)

    def step(t, carry):
        g = t // steps
        i = t % steps
        n = 2 * t

        @pl.when(jnp.logical_and(i == 0, g < groups - 2))
        def _():
            send_old(g + 2).start()

        @pl.when(jnp.logical_and(i == steps - 1, g > 0))
        def _():
            pass_back(g - 1)

        @pl.when(jnp.logical_and(jnp.logical_and(i == steps - 1, g < groups - 1), odd))
        def _():
            forward_old(g + 1)

        scores(n + 1, s_1)
        soften(s_0, w_0)
        results(n - 1, w_1)

        @pl.when(jnp.logical_and(i == 0, g > 0))
        def _():
            finish_group(g - 1)

        @pl.when(jnp.logical_and(i == steps - 1, g < groups - 1))
        def _():
            begin_group(g + 1)

        scores(n + 2, s_0)
        soften(s_1, w_1)
        results(n, w_0)
        return carry

    lax.fori_loop(0, groups * steps, step, 0)
    results(stages - 1, w_1)
    finish_group(groups - 1)
    pass_back(groups - 1)

    for g in range(groups):
        @pl.when(jnp.logical_not(odd))
        def _():
            grad_x(g).wait_recv()
            own[g] += xrcv[g].astype(jnp.float32)

        grad_z(g).wait_recv()
        for i, out in enumerate((gk_vm, gv_vm)):
            out[:, g * D : (g + 1) * D] = (
                own[g, i] + zrcv[g, i].astype(jnp.float32)).astype(jnp.bfloat16)
    for g in range(groups):
        if g:
            send_old(g).wait_send()
        for copy in (send_prev(g), grad_x(g), grad_z(g)):
            copy.wait_send()


def write_out(*refs):
    count = len(refs) // 2
    sems = refs[-1]
    copies = [pltpu.make_async_copy(refs[i], refs[count + i], sems.at[i]) for i in range(count)]
    for copy in copies:
        copy.start()
    for copy in copies:
        copy.wait()


def shards(mesh_shape, query, key_proj, value_projection, upstream, doc_start):
    groups = key_proj.shape[1] // D
    heads = query.shape[1] // D // groups
    bf16, f32 = jnp.bfloat16, jnp.float32
    dma = pltpu.SemaphoreType.DMA
    vm = pltpu.VMEM
    wide = (groups, T, heads * D)
    stage = (R, 2 * S)
    in_hbm = pl.BlockSpec(memory_space=pltpu.HBM)
    in_vmem = pl.BlockSpec(memory_space=pltpu.VMEM)
    shapes = (query.shape, query.shape, key_proj.shape, key_proj.shape)
    args = [
        pltpu.with_memory_space_constraint(x, pltpu.HBM)
        for x in (query, key_proj, value_projection, upstream, doc_start)
    ]
    held = pl.pallas_call(
        functools.partial(kernel, mesh_shape, groups, heads),
        out_shape=tuple(pltpu.VMEM(shape, bf16) for shape in shapes),
        in_specs=[in_hbm] * 5,
        out_specs=(in_vmem,) * 4,
        scratch_shapes=[
            vm(wide, bf16), vm(wide, bf16),
            vm(doc_start.shape, jnp.int32),
            vm((groups, 2, 3 * T, D), bf16),
            vm((groups, 2 * D, 2 * S), bf16), vm((groups, 2 * S, 2 * D), bf16),
            vm((T, T), bf16), vm((T, 2 * T), f32),
            vm(stage, f32), vm(stage, f32), vm(stage, bf16), vm(stage, bf16),
            vm((2, D, 3 * T), f32),
            vm((groups, 2, T, D), f32), vm((groups, 2, T, D), f32),
            vm((groups, 2, T, D), bf16), vm((groups, 2, T, D), bf16),
            vm((groups, 2, T, D), bf16), vm((groups, 2, T, D), bf16),
            dma((groups, 2)), dma, dma((groups, 2)),
            dma((groups,)), dma((groups,)), dma((groups,)), dma((groups,)),
            dma((groups,)), dma((groups,)), dma((groups,)), dma((groups,)),
        ],
        compiler_params=pltpu.CompilerParams(
            collective_id=0, has_side_effects=True, vmem_limit_bytes=40 * 1024 * 1024),
        cost_estimate=pl.CostEstimate(
            flops=12 * query.size * 3 * T, bytes_accessed=8 * query.size,
            transcendentals=query.size * 2),
    )(*args)
    held = [pltpu.with_memory_space_constraint(x, pltpu.VMEM) for x in held]
    return pl.pallas_call(
        write_out,
        out_shape=tuple(pltpu.HBM(shape, bf16) for shape in shapes),
        in_specs=[in_vmem] * 4,
        out_specs=(in_hbm,) * 4,
        scratch_shapes=[dma((4,))],
        compiler_params=pltpu.CompilerParams(vmem_limit_bytes=8 * 1024 * 1024),
    )(*held)


def solution(mesh):
    mesh_shape = (mesh.shape["inner"], mesh.shape["outer"])
    rows = P(("uly", "inner", "outer"), None)
    return jax.shard_map(
        functools.partial(shards, mesh_shape), mesh=mesh,
        in_specs=(rows, rows, rows, rows, P(None, ("inner", "outer"))),
        out_specs=(rows, rows, rows, rows), check_vma=False)
```

```python
import functools
import math

import jax
import jax.numpy as jnp
from jax import lax
from jax.experimental import pallas as pl
from jax.experimental.pallas import tpu as pltpu
from jax.sharding import PartitionSpec as P

MESH = pl.DeviceIdType.MESH
D = 128
T = 128
HEADS = 4
R = HEADS * T
S = 3 * T
ROWS = 128
MASKED = -1e30

NN = (((1,), (0,)), ((), ()))


def dot(a, b):
    return lax.dot_general(a, b, NN, preferred_element_type=jnp.float32)


def kernel(
    mesh_shape, groups, heads,
    q_hbm, k_hbm, v_hbm, up_hbm, st_hbm,
    o_vm, gq_vm, gk_vm, gv_vm,
    q_vm, up_vm, st_vm, kv, fan_in, fan_out, tri, bias,
    s_0, s_1, w_0, w_1, q_t, up_t,
    acc, own, old, xsnd, xrcv, zsnd, zrcv,
    load_sem, st_sem, own_sem, prev_send, prev_recv, old_send, old_recv,
    gx_send, gx_recv, gz_send, gz_recv,
):
    n_inner, n_outer = mesh_shape
    blocks = n_inner * n_outer
    chunks = 4 * blocks
    width = heads * D
    per_group = heads // HEADS
    stages = groups * per_group
    steps = per_group // 2
    scale = D ** -0.5
    rate = scale * math.log2(math.e)

    u = lax.axis_index("uly")
    b = lax.axis_index("inner") * n_outer + lax.axis_index("outer")
    late = u // 2
    half = u - 2 * late
    span = b + late * (2 * blocks - 1 - 2 * b)
    chunk = 2 * span + half
    odd = half == 1

    def device_of(c):
        s = c // 2
        is_late = s // blocks
        blk = s + is_late * (2 * blocks - 1 - 2 * s)
        return (c - 2 * s + 2 * is_late, blk // n_outer, blk % n_outer)

    partner = (u + 1 - 2 * half, lax.axis_index("inner"), lax.axis_index("outer"))
    after = device_of((chunk + 2) % chunks)
    before = device_of((chunk + chunks - 2) % chunks)

    def cols(g):
        return pl.ds(pl.multiple_of(g * width, width), width)

    def load(g):
        return (
            pltpu.make_async_copy(q_hbm.at[:, cols(g)], q_vm.at[g], load_sem.at[g, 0]),
            pltpu.make_async_copy(up_hbm.at[:, cols(g)], up_vm.at[g], load_sem.at[g, 1]),
        )

    def load_own(g):
        return tuple(
            pltpu.make_async_copy(
                src.at[:, pl.ds(g * D, D)], kv.at[g, i, pl.ds(0, T)], own_sem.at[g, i])
            for i, src in enumerate((k_hbm, v_hbm))
        )

    def send_old(g):
        return pltpu.make_async_remote_copy(
            src_ref=kv.at[g, :, pl.ds(0, T)], dst_ref=kv.at[g, :, pl.ds(2 * T, T)],
            send_sem=old_send.at[g], recv_sem=old_recv.at[g],
            device_id=after, device_id_type=MESH)

    def send_prev(g):
        return pltpu.make_async_remote_copy(
            src_ref=kv.at[g, :, pl.ds(pl.multiple_of(half * (2 * T), T), T)],
            dst_ref=kv.at[g, :, pl.ds(T, T)],
            send_sem=prev_send.at[g], recv_sem=prev_recv.at[g],
            device_id=partner, device_id_type=MESH)

    def grad_x(g):
        return pltpu.make_async_remote_copy(
            src_ref=xsnd.at[g], dst_ref=xrcv.at[g], send_sem=gx_send.at[g],
            recv_sem=gx_recv.at[g], device_id=partner, device_id_type=MESH)

    def grad_z(g):
        return pltpu.make_async_remote_copy(
            src_ref=zsnd.at[g], dst_ref=zrcv.at[g], send_sem=gz_send.at[g],
            recv_sem=gz_recv.at[g], device_id=before, device_id_type=MESH)

    barrier = pltpu.get_barrier_semaphore()
    for peer in (partner, after, before):
        pl.semaphore_signal(barrier, inc=1, device_id=peer, device_id_type=MESH)

    starts = pltpu.make_async_copy(st_hbm, st_vm, st_sem)
    for g in range(groups):
        for copy in load_own(g):
            copy.start()
    starts.start()
    for g in range(groups):
        for copy in load(g):
            copy.start()

    for copy in load_own(0):
        copy.wait()
    pl.semaphore_wait(barrier, 3)
    send_old(0).start()

    @pl.when(jnp.logical_not(odd))
    def _():
        send_prev(0).start()

    for g in range(1, groups):
        for copy in load_own(g):
            copy.wait()

    starts.wait()
    first = st_vm[0:1, :]
    for i in range(1, 4):
        first = jnp.where(u == i, st_vm[i : i + 1, :], first)
    first = first - chunk * T
    key_at = lax.broadcasted_iota(jnp.int32, (T, T), 0)
    query_at = lax.broadcasted_iota(jnp.int32, (T, T), 1)
    seen = (
        (key_at <= query_at) & (key_at >= first),
        key_at - T >= first,
        (key_at > query_at) & (key_at - 2 * T >= first),
    )
    near = jnp.where(seen[0] | seen[2], 0.0, MASKED)
    bias[:, :T] = near.T
    bias[:, T:] = jnp.where(seen[1], 0.0, MASKED).T
    tri[...] = jnp.where(key_at >= query_at, 1.0, 0.0).astype(jnp.bfloat16)
    fan_in[...] = jnp.zeros_like(fan_in)
    fan_out[...] = jnp.zeros_like(fan_out)

    def spread(g, lo, hi):
        fan_in[g, :D, lo:hi] = kv[g, 0, lo:hi].T
        fan_in[g, D:, S + lo : S + hi] = kv[g, 1, lo:hi].T
        fan_out[g, lo:hi, :D] = kv[g, 1, lo:hi]
        fan_out[g, S + lo : S + hi, D:] = kv[g, 0, lo:hi]

    for g in range(groups):
        spread(g, 0, T)

    send_old(0).wait_send()
    send_old(1).start()

    @pl.when(jnp.logical_not(odd))
    def _():
        for g in range(1, groups):
            send_prev(g).start()

    def lanes_of(n):
        at = (n % per_group) * R
        return [pl.ds(pl.multiple_of(at + i * D, D), D) for i in range(HEADS)]

    def rows_of(ref, n):
        return jnp.concatenate([ref[n // per_group, :, c] for c in lanes_of(n)], axis=0)

    for g in range(groups):
        for copy in load(g):
            copy.wait()

    def turn(n, carry):
        q_t[n] = rows_of(q_vm, n).T
        up_t[n] = rows_of(up_vm, n).T
        return carry

    lax.fori_loop(0, stages, turn, 0)

    def forward_old(g):
        send_old(g).wait_recv()
        send_prev(g).start()

    @pl.when(odd)
    def _():
        forward_old(0)

    def begin_group(g):
        @pl.when(jnp.logical_not(odd))
        def _():
            send_old(g).wait_recv()

        send_prev(g).wait_recv()
        spread(g, T, S)

    def scores(n, s_out):
        n = jnp.minimum(n, stages - 1)
        both = jnp.concatenate([rows_of(q_vm, n), rows_of(up_vm, n)], axis=1)
        s_out[...] = dot(both, fan_in[n // per_group])

    def soften(s_ref, w_out, t):
        for at in range(0, R, ROWS):
            rows = slice(at, at + ROWS)
            own_k, mid_k, old_k = [slice(i * T, (i + 1) * T) for i in range(3)]
            own_v, mid_v, old_v = [slice(i * T, (i + 1) * T) for i in range(3, 6)]
            here = slice(at % T, at % T + ROWS)
            key_at = lax.broadcasted_iota(jnp.int32, (ROWS, T), 1)
            query_at = lax.broadcasted_iota(jnp.int32, (ROWS, T), 0) + at % T
            lower = key_at <= query_at
            s_mix = jnp.where(lower, s_ref[rows, own_k], s_ref[rows, old_k]) + bias[here, :T]
            s_mid = s_ref[rows, mid_k] + bias[here, T:]
            top = jnp.max(jnp.maximum(s_mix, s_mid), axis=1, keepdims=True)
            e_mix = jnp.exp2((s_mix - top) * rate)
            e_mid = jnp.exp2((s_mid - top) * rate)
            inverse = 1.0 / jnp.sum(e_mix + e_mid, axis=1, keepdims=True)
            dp_mix = jnp.where(lower, s_ref[rows, own_v], s_ref[rows, old_v])
            dp_mid = s_ref[rows, mid_v]
            w_mix = e_mix * inverse
            w_mid = e_mid * inverse
            delta = jnp.sum(w_mix * dp_mix + w_mid * dp_mid, axis=1, keepdims=True)
            ds_mix = w_mix * (dp_mix - delta)
            ds_mid = w_mid * (dp_mid - delta)
            for mix, mid, base in ((w_mix, w_mid, 0), (ds_mix, ds_mid, S)):
                mix = mix.astype(jnp.bfloat16)
                own_part = mix * tri[here, :]
                w_out[t, rows, base : base + T] = own_part
                w_out[t, rows, base + T : base + 2 * T] = mid.astype(jnp.bfloat16)
                w_out[t, rows, base + 2 * T : base + S] = mix - own_part

    def key_results(n, w_ref, t):
        n = jnp.maximum(n, 0)
        t = jnp.maximum(t, 0)
        acc[1] += dot(up_t[n], w_ref[t, :, :S])
        acc[0] += dot(q_t[n], w_ref[t, :, S:])

    def row_results(n, w_ref, t):
        both = dot(w_ref[t], fan_out[n // per_group])
        for i in range(HEADS):
            lanes = pl.ds(pl.multiple_of(n * R + i * D, D), D)
            rows = slice(i * T, (i + 1) * T)
            o_vm[:, lanes] = both[rows, :D].astype(jnp.bfloat16)
            gq_vm[:, lanes] = (both[rows, D:] * scale).astype(jnp.bfloat16)

    def finish_group(g):
        for i in range(2):
            grad = acc[i] * scale if i == 0 else acc[i]
            own[g, i] = grad[:, :T].T
            xsnd[g, i] = grad[:, T : 2 * T].T.astype(jnp.bfloat16)
            old[g, i] = grad[:, 2 * T :].T
        acc[...] = jnp.zeros_like(acc)
        grad_x(g).start()

        @pl.when(jnp.logical_not(odd))
        def _():
            zsnd[g] = old[g].astype(jnp.bfloat16)
            grad_z(g).start()

    def pass_back(g):
        @pl.when(odd)
        def _():
            grad_x(g).wait_recv()
            zsnd[g] = (old[g] + xrcv[g].astype(jnp.float32)).astype(jnp.bfloat16)
            grad_z(g).start()

    begin_group(0)
    acc[...] = jnp.zeros_like(acc)
    w_1[0] = jnp.zeros(w_1.shape[1:], w_1.dtype)
    scores(0, s_0)

    def step(t, carry):
        g = t // steps
        i = t % steps
        n = 2 * t

        @pl.when(jnp.logical_and(i == 0, g < groups - 2))
        def _():
            send_old(g + 2).start()

        @pl.when(jnp.logical_and(i == steps - 1, g > 0))
        def _():
            pass_back(g - 1)

        @pl.when(jnp.logical_and(jnp.logical_and(i == steps - 1, g < groups - 1), odd))
        def _():
            forward_old(g + 1)

        scores(n + 1, s_1)
        soften(s_0, w_0, t)
        key_results(n - 1, w_1, t - 1)

        @pl.when(jnp.logical_and(i == 0, g > 0))
        def _():
            finish_group(g - 1)

        @pl.when(jnp.logical_and(i == steps - 1, g < groups - 1))
        def _():
            begin_group(g + 1)

        scores(n + 2, s_0)
        soften(s_1, w_1, t)
        key_results(n, w_0, t)
        return carry

    lax.fori_loop(0, groups * steps, step, 0)
    key_results(stages - 1, w_1, stages // 2 - 1)
    finish_group(groups - 1)

    def rest(t, carry):
        row_results(2 * t, w_0, t)
        row_results(2 * t + 1, w_1, t)

        @pl.when(t == 2)
        def _():
            pass_back(groups - 1)

        return carry

    lax.fori_loop(0, stages // 2, rest, 0)

    for g in range(groups):
        @pl.when(jnp.logical_not(odd))
        def _():
            grad_x(g).wait_recv()
            own[g] += xrcv[g].astype(jnp.float32)

        grad_z(g).wait_recv()
        for i, out in enumerate((gk_vm, gv_vm)):
            out[:, g * D : (g + 1) * D] = (
                own[g, i] + zrcv[g, i].astype(jnp.float32)).astype(jnp.bfloat16)
    for g in range(groups):
        if g:
            send_old(g).wait_send()
        for copy in (send_prev(g), grad_x(g), grad_z(g)):
            copy.wait_send()


def write_out(*refs):
    count = len(refs) // 2
    sems = refs[-1]
    copies = [pltpu.make_async_copy(refs[i], refs[count + i], sems.at[i]) for i in range(count)]
    for copy in copies:
        copy.start()
    for copy in copies:
        copy.wait()


def shards(mesh_shape, query, key_proj, value_projection, upstream, doc_start):
    groups = key_proj.shape[1] // D
    heads = query.shape[1] // D // groups
    bf16, f32 = jnp.bfloat16, jnp.float32
    dma = pltpu.SemaphoreType.DMA
    vm = pltpu.VMEM
    wide = (groups, T, heads * D)
    stage = (R, 2 * S)
    stages = groups * heads // HEADS
    half = (stages // 2,) + stage
    turned = (stages, D, R)
    in_hbm = pl.BlockSpec(memory_space=pltpu.HBM)
    in_vmem = pl.BlockSpec(memory_space=pltpu.VMEM)
    shapes = (query.shape, query.shape, key_proj.shape, key_proj.shape)
    args = [
        pltpu.with_memory_space_constraint(x, pltpu.HBM)
        for x in (query, key_proj, value_projection, upstream, doc_start)
    ]
    held = pl.pallas_call(
        functools.partial(kernel, mesh_shape, groups, heads),
        out_shape=tuple(pltpu.VMEM(shape, bf16) for shape in shapes),
        in_specs=[in_hbm] * 5,
        out_specs=(in_vmem,) * 4,
        scratch_shapes=[
            vm(wide, bf16), vm(wide, bf16),
            vm(doc_start.shape, jnp.int32),
            vm((groups, 2, 3 * T, D), bf16),
            vm((groups, 2 * D, 2 * S), bf16), vm((groups, 2 * S, 2 * D), bf16),
            vm((T, T), bf16), vm((T, 2 * T), f32),
            vm(stage, f32), vm(stage, f32), vm(half, bf16), vm(half, bf16), vm(turned, bf16), vm(turned, bf16),
            vm((2, D, 3 * T), f32),
            vm((groups, 2, T, D), f32), vm((groups, 2, T, D), f32),
            vm((groups, 2, T, D), bf16), vm((groups, 2, T, D), bf16),
            vm((groups, 2, T, D), bf16), vm((groups, 2, T, D), bf16),
            dma((groups, 2)), dma, dma((groups, 2)),
            dma((groups,)), dma((groups,)), dma((groups,)), dma((groups,)),
            dma((groups,)), dma((groups,)), dma((groups,)), dma((groups,)),
        ],
        compiler_params=pltpu.CompilerParams(
            collective_id=0, has_side_effects=True, vmem_limit_bytes=48 * 1024 * 1024),
        cost_estimate=pl.CostEstimate(
            flops=12 * query.size * 3 * T, bytes_accessed=8 * query.size,
            transcendentals=query.size * 2),
    )(*args)
    held = [pltpu.with_memory_space_constraint(x, pltpu.VMEM) for x in held]
    return pl.pallas_call(
        write_out,
        out_shape=tuple(pltpu.HBM(shape, bf16) for shape in shapes),
        in_specs=[in_vmem] * 4,
        out_specs=(in_hbm,) * 4,
        scratch_shapes=[dma((4,))],
        compiler_params=pltpu.CompilerParams(vmem_limit_bytes=8 * 1024 * 1024),
    )(*held)


def solution(mesh):
    mesh_shape = (mesh.shape["inner"], mesh.shape["outer"])
    rows = P(("uly", "inner", "outer"), None)
    return jax.shard_map(
        functools.partial(shards, mesh_shape), mesh=mesh,
        in_specs=(rows, rows, rows, rows, P(None, ("inner", "outer"))),
        out_specs=(rows, rows, rows, rows), check_vma=False)
```

```python
import functools
import math

import jax
import jax.numpy as jnp
from jax import lax
from jax.experimental import pallas as pl
from jax.experimental.pallas import tpu as pltpu
from jax.sharding import PartitionSpec as P

MESH = pl.DeviceIdType.MESH
D = 128
T = 128
HEADS = 4
R = HEADS * T
S = 3 * T
ROWS = 128
MASKED = -1e30

NN = (((1,), (0,)), ((), ()))


def dot(a, b):
    return lax.dot_general(a, b, NN, preferred_element_type=jnp.float32)


def kernel(
    mesh_shape, groups, heads,
    q_hbm, k_hbm, v_hbm, up_hbm, st_hbm,
    o_out, gq_out, gk_out, gv_out,
    q_vm, up_vm, o_vm, gq_vm, gk_vm, gv_vm, st_vm, kv, fan_in, fan_out, tri, bias,
    s_0, s_1, w_0, w_1, q_t, up_t,
    acc, own, old, xsnd, xrcv, zsnd, zrcv,
    load_sem, st_sem, own_sem, prev_send, prev_recv, old_send, old_recv,
    gx_send, gx_recv, gz_send, gz_recv, out_sem, gout_sem,
):
    n_inner, n_outer = mesh_shape
    blocks = n_inner * n_outer
    chunks = 4 * blocks
    width = heads * D
    per_group = heads // HEADS
    stages = groups * per_group
    steps = per_group // 2
    scale = D ** -0.5
    rate = scale * math.log2(math.e)

    u = lax.axis_index("uly")
    b = lax.axis_index("inner") * n_outer + lax.axis_index("outer")
    late = u // 2
    half = u - 2 * late
    span = b + late * (2 * blocks - 1 - 2 * b)
    chunk = 2 * span + half
    odd = half == 1

    def device_of(c):
        s = c // 2
        is_late = s // blocks
        blk = s + is_late * (2 * blocks - 1 - 2 * s)
        return (c - 2 * s + 2 * is_late, blk // n_outer, blk % n_outer)

    partner = (u + 1 - 2 * half, lax.axis_index("inner"), lax.axis_index("outer"))
    after = device_of((chunk + 2) % chunks)
    before = device_of((chunk + chunks - 2) % chunks)

    def cols(g):
        return pl.ds(pl.multiple_of(g * width, width), width)

    def load(g):
        return (
            pltpu.make_async_copy(q_hbm.at[:, cols(g)], q_vm.at[g], load_sem.at[g, 0]),
            pltpu.make_async_copy(up_hbm.at[:, cols(g)], up_vm.at[g], load_sem.at[g, 1]),
        )

    def store(g):
        return (
            pltpu.make_async_copy(o_vm.at[g], o_out.at[:, cols(g)], out_sem.at[g, 0]),
            pltpu.make_async_copy(gq_vm.at[g], gq_out.at[:, cols(g)], out_sem.at[g, 1]),
        )

    def load_own(g):
        return tuple(
            pltpu.make_async_copy(
                src.at[:, pl.ds(g * D, D)], kv.at[g, i, pl.ds(0, T)], own_sem.at[g, i])
            for i, src in enumerate((k_hbm, v_hbm))
        )

    def send_old(g):
        return pltpu.make_async_remote_copy(
            src_ref=kv.at[g, :, pl.ds(0, T)], dst_ref=kv.at[g, :, pl.ds(2 * T, T)],
            send_sem=old_send.at[g], recv_sem=old_recv.at[g],
            device_id=after, device_id_type=MESH)

    def send_prev(g):
        return pltpu.make_async_remote_copy(
            src_ref=kv.at[g, :, pl.ds(pl.multiple_of(half * (2 * T), T), T)],
            dst_ref=kv.at[g, :, pl.ds(T, T)],
            send_sem=prev_send.at[g], recv_sem=prev_recv.at[g],
            device_id=partner, device_id_type=MESH)

    def grad_x(g):
        return pltpu.make_async_remote_copy(
            src_ref=xsnd.at[g], dst_ref=xrcv.at[g], send_sem=gx_send.at[g],
            recv_sem=gx_recv.at[g], device_id=partner, device_id_type=MESH)

    def grad_z(g):
        return pltpu.make_async_remote_copy(
            src_ref=zsnd.at[g], dst_ref=zrcv.at[g], send_sem=gz_send.at[g],
            recv_sem=gz_recv.at[g], device_id=before, device_id_type=MESH)

    barrier = pltpu.get_barrier_semaphore()
    for peer in (partner, after, before):
        pl.semaphore_signal(barrier, inc=1, device_id=peer, device_id_type=MESH)

    starts = pltpu.make_async_copy(st_hbm, st_vm, st_sem)
    for g in range(groups):
        for copy in load_own(g):
            copy.start()
    starts.start()
    for g in range(groups):
        for copy in load(g):
            copy.start()

    for copy in load_own(0):
        copy.wait()
    pl.semaphore_wait(barrier, 3)
    send_old(0).start()

    @pl.when(jnp.logical_not(odd))
    def _():
        send_prev(0).start()

    for g in range(1, groups):
        for copy in load_own(g):
            copy.wait()

    starts.wait()
    first = st_vm[0:1, :]
    for i in range(1, 4):
        first = jnp.where(u == i, st_vm[i : i + 1, :], first)
    first = first - chunk * T
    key_at = lax.broadcasted_iota(jnp.int32, (T, T), 0)
    query_at = lax.broadcasted_iota(jnp.int32, (T, T), 1)
    seen = (
        (key_at <= query_at) & (key_at >= first),
        key_at - T >= first,
        (key_at > query_at) & (key_at - 2 * T >= first),
    )
    near = jnp.where(seen[0] | seen[2], 0.0, MASKED)
    bias[:, :T] = near.T
    bias[:, T:] = jnp.where(seen[1], 0.0, MASKED).T
    tri[...] = jnp.where(key_at >= query_at, 1.0, 0.0).astype(jnp.bfloat16)
    fan_in[...] = jnp.zeros_like(fan_in)
    fan_out[...] = jnp.zeros_like(fan_out)

    def spread(g, lo, hi):
        fan_in[g, :D, lo:hi] = kv[g, 0, lo:hi].T
        fan_in[g, D:, S + lo : S + hi] = kv[g, 1, lo:hi].T
        fan_out[g, lo:hi, :D] = kv[g, 1, lo:hi]
        fan_out[g, S + lo : S + hi, D:] = kv[g, 0, lo:hi]

    for g in range(groups):
        spread(g, 0, T)

    send_old(1).start()

    @pl.when(jnp.logical_not(odd))
    def _():
        for g in range(1, groups):
            send_prev(g).start()

    def lanes_of(n):
        at = (n % per_group) * R
        return [pl.ds(pl.multiple_of(at + i * D, D), D) for i in range(HEADS)]

    def rows_of(ref, n):
        return jnp.concatenate([ref[n // per_group, :, c] for c in lanes_of(n)], axis=0)

    def turn(n, carry):
        q_t[n] = rows_of(q_vm, n).T
        up_t[n] = rows_of(up_vm, n).T
        return carry

    for g in range(groups):
        for copy in load(g):
            copy.wait()
        lax.fori_loop(g * per_group, (g + 1) * per_group, turn, 0)
        if g + 2 < groups:
            send_old(g + 2).start()

    def forward_old(g):
        send_old(g).wait_recv()
        send_prev(g).start()

    @pl.when(odd)
    def _():
        forward_old(0)

    def begin_group(g):
        @pl.when(jnp.logical_not(odd))
        def _():
            send_old(g).wait_recv()

        send_prev(g).wait_recv()
        spread(g, T, S)

    def scores(n, s_out):
        n = jnp.minimum(n, stages - 1)
        both = jnp.concatenate([rows_of(q_vm, n), rows_of(up_vm, n)], axis=1)
        s_out[...] = dot(both, fan_in[n // per_group])

    def soften(s_ref, w_out, t):
        for at in range(0, R, ROWS):
            rows = slice(at, at + ROWS)
            own_k, mid_k, old_k = [slice(i * T, (i + 1) * T) for i in range(3)]
            own_v, mid_v, old_v = [slice(i * T, (i + 1) * T) for i in range(3, 6)]
            here = slice(at % T, at % T + ROWS)
            key_at = lax.broadcasted_iota(jnp.int32, (ROWS, T), 1)
            query_at = lax.broadcasted_iota(jnp.int32, (ROWS, T), 0) + at % T
            lower = key_at <= query_at
            s_mix = jnp.where(lower, s_ref[rows, own_k], s_ref[rows, old_k]) + bias[here, :T]
            s_mid = s_ref[rows, mid_k] + bias[here, T:]
            top = jnp.max(jnp.maximum(s_mix, s_mid), axis=1, keepdims=True)
            e_mix = jnp.exp2((s_mix - top) * rate)
            e_mid = jnp.exp2((s_mid - top) * rate)
            inverse = 1.0 / jnp.sum(e_mix + e_mid, axis=1, keepdims=True)
            dp_mix = jnp.where(lower, s_ref[rows, own_v], s_ref[rows, old_v])
            dp_mid = s_ref[rows, mid_v]
            w_mix = e_mix * inverse
            w_mid = e_mid * inverse
            delta = jnp.sum(w_mix * dp_mix + w_mid * dp_mid, axis=1, keepdims=True)
            ds_mix = w_mix * (dp_mix - delta)
            ds_mid = w_mid * (dp_mid - delta)
            for mix, mid, base in ((w_mix, w_mid, 0), (ds_mix, ds_mid, S)):
                mix = mix.astype(jnp.bfloat16)
                own_part = mix * tri[here, :]
                w_out[t, rows, base : base + T] = own_part
                w_out[t, rows, base + T : base + 2 * T] = mid.astype(jnp.bfloat16)
                w_out[t, rows, base + 2 * T : base + S] = mix - own_part

    def key_results(n, w_ref, t):
        n = jnp.maximum(n, 0)
        t = jnp.maximum(t, 0)
        acc[1] += dot(up_t[n], w_ref[t, :, :S])
        acc[0] += dot(q_t[n], w_ref[t, :, S:])

    def row_results(n, w_ref, t):
        g = n // per_group
        both = dot(w_ref[t], fan_out[g])
        for i, lanes in enumerate(lanes_of(n)):
            rows = slice(i * T, (i + 1) * T)
            o_vm[g, :, lanes] = both[rows, :D].astype(jnp.bfloat16)
            gq_vm[g, :, lanes] = (both[rows, D:] * scale).astype(jnp.bfloat16)

    def finish_group(g):
        for i in range(2):
            grad = acc[i] * scale if i == 0 else acc[i]
            own[g, i] = grad[:, :T].T
            xsnd[g, i] = grad[:, T : 2 * T].T.astype(jnp.bfloat16)
            old[g, i] = grad[:, 2 * T :].T
        acc[...] = jnp.zeros_like(acc)
        grad_x(g).start()

        @pl.when(jnp.logical_not(odd))
        def _():
            zsnd[g] = old[g].astype(jnp.bfloat16)
            grad_z(g).start()

    def pass_back(g):
        @pl.when(odd)
        def _():
            grad_x(g).wait_recv()
            zsnd[g] = (old[g] + xrcv[g].astype(jnp.float32)).astype(jnp.bfloat16)
            grad_z(g).start()

    begin_group(0)
    acc[...] = jnp.zeros_like(acc)
    w_1[0] = jnp.zeros(w_1.shape[1:], w_1.dtype)
    scores(0, s_0)

    def step(t, carry):
        g = t // steps
        i = t % steps
        n = 2 * t

        @pl.when(jnp.logical_and(i == steps - 1, g > 0))
        def _():
            pass_back(g - 1)

        @pl.when(jnp.logical_and(jnp.logical_and(i == steps - 1, g < groups - 1), odd))
        def _():
            forward_old(g + 1)

        scores(n + 1, s_1)
        soften(s_0, w_0, t)
        key_results(n - 1, w_1, t - 1)

        @pl.when(jnp.logical_and(i == 0, g > 0))
        def _():
            finish_group(g - 1)

        @pl.when(jnp.logical_and(i == steps - 1, g < groups - 1))
        def _():
            begin_group(g + 1)

        scores(n + 2, s_0)
        soften(s_1, w_1, t)
        key_results(n, w_0, t)
        return carry

    lax.fori_loop(0, groups * steps, step, 0)
    key_results(stages - 1, w_1, stages // 2 - 1)
    finish_group(groups - 1)

    def rest(t, carry):
        row_results(2 * t, w_0, t)
        row_results(2 * t + 1, w_1, t)

        @pl.when(t % steps == steps - 1)
        def _():
            for copy in store(t // steps):
                copy.start()

        @pl.when(t == 2)
        def _():
            pass_back(groups - 1)

        return carry

    lax.fori_loop(0, stages // 2, rest, 0)

    for g in range(groups):
        @pl.when(jnp.logical_not(odd))
        def _():
            grad_x(g).wait_recv()
            own[g] += xrcv[g].astype(jnp.float32)

        grad_z(g).wait_recv()
        for i, out in enumerate((gk_vm, gv_vm)):
            out[:, g * D : (g + 1) * D] = (
                own[g, i] + zrcv[g, i].astype(jnp.float32)).astype(jnp.bfloat16)
    outs = [
        pltpu.make_async_copy(src, dst, gout_sem.at[i])
        for i, (src, dst) in enumerate(((gk_vm, gk_out), (gv_vm, gv_out)))
    ]
    for copy in outs:
        copy.start()
    for g in range(groups):
        for copy in store(g):
            copy.wait()
    for copy in outs:
        copy.wait()
    for g in range(groups):
        for copy in (send_old(g), send_prev(g), grad_x(g), grad_z(g)):
            copy.wait_send()


def write_out(*refs):
    count = len(refs) // 2
    sems = refs[-1]
    copies = [pltpu.make_async_copy(refs[i], refs[count + i], sems.at[i]) for i in range(count)]
    for copy in copies:
        copy.start()
    for copy in copies:
        copy.wait()


def shards(mesh_shape, query, key_proj, value_projection, upstream, doc_start):
    groups = key_proj.shape[1] // D
    heads = query.shape[1] // D // groups
    bf16, f32 = jnp.bfloat16, jnp.float32
    dma = pltpu.SemaphoreType.DMA
    vm = pltpu.VMEM
    wide = (groups, T, heads * D)
    stage = (R, 2 * S)
    stages = groups * heads // HEADS
    half = (stages // 2,) + stage
    turned = (stages, D, R)
    in_hbm = pl.BlockSpec(memory_space=pltpu.HBM)
    anywhere = pl.BlockSpec(memory_space=pl.ANY)
    shapes = (query.shape, query.shape, key_proj.shape, key_proj.shape)
    args = [
        pltpu.with_memory_space_constraint(x, pltpu.HBM)
        for x in (query, key_proj, value_projection, upstream, doc_start)
    ]
    held = pl.pallas_call(
        functools.partial(kernel, mesh_shape, groups, heads),
        out_shape=tuple(pltpu.VMEM(shape, bf16) for shape in shapes),
        in_specs=[in_hbm] * 5,
        out_specs=(anywhere,) * 4,
        scratch_shapes=[
            vm(wide, bf16), vm(wide, bf16), vm(wide, bf16), vm(wide, bf16),
            vm(key_proj.shape, bf16), vm(key_proj.shape, bf16),
            vm(doc_start.shape, jnp.int32),
            vm((groups, 2, 3 * T, D), bf16),
            vm((groups, 2 * D, 2 * S), bf16), vm((groups, 2 * S, 2 * D), bf16),
            vm((T, T), bf16), vm((T, 2 * T), f32),
            vm(stage, f32), vm(stage, f32), vm(half, bf16), vm(half, bf16), vm(turned, bf16), vm(turned, bf16),
            vm((2, D, 3 * T), f32),
            vm((groups, 2, T, D), f32), vm((groups, 2, T, D), f32),
            vm((groups, 2, T, D), bf16), vm((groups, 2, T, D), bf16),
            vm((groups, 2, T, D), bf16), vm((groups, 2, T, D), bf16),
            dma((groups, 2)), dma, dma((groups, 2)),
            dma((groups,)), dma((groups,)), dma((groups,)), dma((groups,)),
            dma((groups,)), dma((groups,)), dma((groups,)), dma((groups,)),
            dma((groups, 2)), dma((2,)),
        ],
        compiler_params=pltpu.CompilerParams(
            collective_id=0, has_side_effects=True, vmem_limit_bytes=48 * 1024 * 1024),
        cost_estimate=pl.CostEstimate(
            flops=12 * query.size * 3 * T, bytes_accessed=8 * query.size,
            transcendentals=query.size * 2),
    )(*args)
    held = [pltpu.with_memory_space_constraint(x, pltpu.VMEM) for x in held]
    return pl.pallas_call(
        write_out,
        out_shape=tuple(pltpu.HBM(shape, bf16) for shape in shapes),
        in_specs=[anywhere] * 4,
        out_specs=(in_hbm,) * 4,
        scratch_shapes=[dma((4,))],
        compiler_params=pltpu.CompilerParams(vmem_limit_bytes=8 * 1024 * 1024),
    )(*held)


def solution(mesh):
    mesh_shape = (mesh.shape["inner"], mesh.shape["outer"])
    rows = P(("uly", "inner", "outer"), None)
    return jax.shard_map(
        functools.partial(shards, mesh_shape), mesh=mesh,
        in_specs=(rows, rows, rows, rows, P(None, ("inner", "outer"))),
        out_specs=(rows, rows, rows, rows), check_vma=False)
```

```python
import functools
import math

import jax
import jax.numpy as jnp
from jax import lax
from jax.experimental import pallas as pl
from jax.experimental.pallas import tpu as pltpu
from jax.sharding import PartitionSpec as P

MESH = pl.DeviceIdType.MESH
D = 128
T = 128
HEADS = 4
R = HEADS * T
S = 3 * T
ROWS = 128
MASKED = -1e30

NN = (((1,), (0,)), ((), ()))


def dot(a, b):
    return lax.dot_general(a, b, NN, preferred_element_type=jnp.float32)


class Place:
    def __init__(self, mesh_shape):
        n_inner, n_outer = mesh_shape
        blocks = n_inner * n_outer
        self.chunks = 4 * blocks
        self.u = u = lax.axis_index("uly")
        b = lax.axis_index("inner") * n_outer + lax.axis_index("outer")
        late = u // 2
        self.half = u - 2 * late
        span = b + late * (2 * blocks - 1 - 2 * b)
        self.chunk = 2 * span + self.half
        self.odd = self.half == 1

        def device_of(c):
            at = c // 2
            is_late = at // blocks
            blk = at + is_late * (2 * blocks - 1 - 2 * at)
            return (c - 2 * at + 2 * is_late, blk // n_outer, blk % n_outer)

        self.partner = (u + 1 - 2 * self.half, lax.axis_index("inner"), lax.axis_index("outer"))
        self.after = device_of((self.chunk + 2) % self.chunks)
        self.before = device_of((self.chunk + self.chunks - 2) % self.chunks)

    def greet(self):
        barrier = pltpu.get_barrier_semaphore()
        for peer in (self.partner, self.after, self.before):
            pl.semaphore_signal(barrier, inc=1, device_id=peer, device_id_type=MESH)

    def wait(self):
        pl.semaphore_wait(pltpu.get_barrier_semaphore(), 3)


def gather(
    mesh_shape, groups, heads, k_hbm, v_hbm, q_hbm, up_hbm, st_hbm,
    q_vm, up_vm, q_t, up_t, fan_in, fan_out, tri, bias,
    kv, st_vm, own_sem, load_sem, st_sem, prev_send, prev_recv, old_send, old_recv,
):
    at = Place(mesh_shape)
    width = heads * D
    per_group = heads // HEADS
    at.greet()
    own = [
        pltpu.make_async_copy(
            src.at[:, pl.ds(g * D, D)], kv.at[g, i, pl.ds(0, T)], own_sem.at[g, i])
        for g in range(groups) for i, src in enumerate((k_hbm, v_hbm))
    ]
    starts = pltpu.make_async_copy(st_hbm, st_vm, st_sem)
    loads = [
        [
            pltpu.make_async_copy(
                src.at[:, pl.ds(g * width, width)], dst.at[g], load_sem.at[g, i])
            for i, (src, dst) in enumerate(((q_hbm, q_vm), (up_hbm, up_vm)))
        ]
        for g in range(groups)
    ]
    for copy in own + [starts] + sum(loads, []):
        copy.start()

    def send_old(g):
        return pltpu.make_async_remote_copy(
            src_ref=kv.at[g, :, pl.ds(0, T)], dst_ref=kv.at[g, :, pl.ds(2 * T, T)],
            send_sem=old_send.at[g], recv_sem=old_recv.at[g],
            device_id=at.after, device_id_type=MESH)

    def send_prev(g):
        return pltpu.make_async_remote_copy(
            src_ref=kv.at[g, :, pl.ds(pl.multiple_of(at.half * (2 * T), T), T)],
            dst_ref=kv.at[g, :, pl.ds(T, T)],
            send_sem=prev_send.at[g], recv_sem=prev_recv.at[g],
            device_id=at.partner, device_id_type=MESH)

    for copy in own:
        copy.wait()
    at.wait()
    for g in range(groups):
        send_old(g).start()

    @pl.when(jnp.logical_not(at.odd))
    def _():
        for g in range(groups):
            send_prev(g).start()

    starts.wait()
    u, chunk = at.u, at.chunk
    first = st_vm[0:1, :]
    for i in range(1, 4):
        first = jnp.where(u == i, st_vm[i : i + 1, :], first)
    first = first - chunk * T
    key_at = lax.broadcasted_iota(jnp.int32, (T, T), 0)
    query_at = lax.broadcasted_iota(jnp.int32, (T, T), 1)
    seen = (
        (key_at <= query_at) & (key_at >= first),
        key_at - T >= first,
        (key_at > query_at) & (key_at - 2 * T >= first),
    )
    near = jnp.where(seen[0] | seen[2], 0.0, MASKED)
    bias[:, :T] = near.T
    bias[:, T:] = jnp.where(seen[1], 0.0, MASKED).T
    tri[...] = jnp.where(key_at >= query_at, 1.0, 0.0).astype(jnp.bfloat16)
    fan_in[...] = jnp.zeros_like(fan_in)
    fan_out[...] = jnp.zeros_like(fan_out)

    def spread(g, lo, hi):
        fan_in[g, :D, lo:hi] = kv[g, 0, lo:hi].T
        fan_in[g, D:, S + lo : S + hi] = kv[g, 1, lo:hi].T
        fan_out[g, lo:hi, :D] = kv[g, 1, lo:hi]
        fan_out[g, S + lo : S + hi, D:] = kv[g, 0, lo:hi]

    for g in range(groups):
        spread(g, 0, T)

    def lanes_of(n):
        at = (n % per_group) * R
        return [pl.ds(pl.multiple_of(at + i * D, D), D) for i in range(HEADS)]

    def rows_of(ref, n):
        return jnp.concatenate([ref[n // per_group, :, c] for c in lanes_of(n)], axis=0)

    def turn(n, carry):
        q_t[n] = rows_of(q_vm, n).T
        up_t[n] = rows_of(up_vm, n).T
        return carry

    for g in range(groups):
        for copy in loads[g]:
            copy.wait()
        lax.fori_loop(g * per_group, (g + 1) * per_group, turn, 0)

    @pl.when(at.odd)
    def _():
        for g in range(groups):
            send_old(g).wait_recv()
            send_prev(g).start()

    @pl.when(jnp.logical_not(at.odd))
    def _():
        for g in range(groups):
            send_old(g).wait_recv()

    for g in range(groups):
        spread(g, 2 * T, S)
    for g in range(groups):
        send_prev(g).wait_recv()
        spread(g, T, 2 * T)
    for g in range(groups):
        send_prev(g).wait_send()
        send_old(g).wait_send()


def attend(
    groups, heads, q_vm, up_vm, q_t, up_t, fan_in, tri, bias, w_0, w_1, grads, s_0, s_1, acc,
):
    per_group = heads // HEADS
    stages = groups * per_group
    steps = per_group // 2
    scale = D ** -0.5
    rate = scale * math.log2(math.e)

    def lanes_of(n):
        at = (n % per_group) * R
        return [pl.ds(pl.multiple_of(at + i * D, D), D) for i in range(HEADS)]

    def rows_of(ref, n):
        return jnp.concatenate([ref[n // per_group, :, c] for c in lanes_of(n)], axis=0)

    def scores(n, s_out):
        n = jnp.minimum(n, stages - 1)
        both = jnp.concatenate([rows_of(q_vm, n), rows_of(up_vm, n)], axis=1)
        s_out[...] = dot(both, fan_in[n // per_group])

    def soften(s_ref, w_out, t):
        for at in range(0, R, ROWS):
            rows = slice(at, at + ROWS)
            own_k, mid_k, old_k = [slice(i * T, (i + 1) * T) for i in range(3)]
            own_v, mid_v, old_v = [slice(i * T, (i + 1) * T) for i in range(3, 6)]
            here = slice(at % T, at % T + ROWS)
            key_at = lax.broadcasted_iota(jnp.int32, (ROWS, T), 1)
            query_at = lax.broadcasted_iota(jnp.int32, (ROWS, T), 0) + at % T
            lower = key_at <= query_at
            s_mix = jnp.where(lower, s_ref[rows, own_k], s_ref[rows, old_k]) + bias[here, :T]
            s_mid = s_ref[rows, mid_k] + bias[here, T:]
            top = jnp.max(jnp.maximum(s_mix, s_mid), axis=1, keepdims=True)
            e_mix = jnp.exp2((s_mix - top) * rate)
            e_mid = jnp.exp2((s_mid - top) * rate)
            inverse = 1.0 / jnp.sum(e_mix + e_mid, axis=1, keepdims=True)
            dp_mix = jnp.where(lower, s_ref[rows, own_v], s_ref[rows, old_v])
            dp_mid = s_ref[rows, mid_v]
            w_mix = e_mix * inverse
            w_mid = e_mid * inverse
            delta = jnp.sum(w_mix * dp_mix + w_mid * dp_mid, axis=1, keepdims=True)
            ds_mix = w_mix * (dp_mix - delta)
            ds_mid = w_mid * (dp_mid - delta)
            for mix, mid, base in ((w_mix, w_mid, 0), (ds_mix, ds_mid, S)):
                mix = mix.astype(jnp.bfloat16)
                own_part = mix * tri[here, :]
                w_out[t, rows, base : base + T] = own_part
                w_out[t, rows, base + T : base + 2 * T] = mid.astype(jnp.bfloat16)
                w_out[t, rows, base + 2 * T : base + S] = mix - own_part

    def key_results(n, w_ref, t):
        n = jnp.maximum(n, 0)
        t = jnp.maximum(t, 0)
        acc[1] += dot(up_t[n], w_ref[t, :, :S])
        acc[0] += dot(q_t[n], w_ref[t, :, S:])

    def finish_group(g):
        for i in range(2):
            grads[g, i] = (acc[i] * scale if i == 0 else acc[i]).T
        acc[...] = jnp.zeros_like(acc)

    acc[...] = jnp.zeros_like(acc)
    w_1[0] = jnp.zeros(w_1.shape[1:], w_1.dtype)
    scores(0, s_0)

    def step(t, carry):
        g = t // steps
        n = 2 * t

        scores(n + 1, s_1)
        soften(s_0, w_0, t)
        key_results(n - 1, w_1, t - 1)

        @pl.when(jnp.logical_and(t % steps == 0, g > 0))
        def _():
            finish_group(g - 1)

        scores(n + 2, s_0)
        soften(s_1, w_1, t)
        key_results(n, w_0, t)
        return carry

    lax.fori_loop(0, groups * steps, step, 0)
    key_results(stages - 1, w_1, stages // 2 - 1)
    finish_group(groups - 1)


def scatter(
    mesh_shape, groups, heads, grads, w_0, w_1, fan_out,
    o_vm, gq_vm, gk_vm, gv_vm, xsnd, xrcv, zsnd, zrcv, gx_send, gx_recv, gz_send, gz_recv,
):
    at = Place(mesh_shape)
    per_group = heads // HEADS
    stages = groups * per_group
    scale = D ** -0.5
    at.greet()

    def grad_x(g):
        return pltpu.make_async_remote_copy(
            src_ref=xsnd.at[g], dst_ref=xrcv.at[g], send_sem=gx_send.at[g],
            recv_sem=gx_recv.at[g], device_id=at.partner, device_id_type=MESH)

    def grad_z(g):
        return pltpu.make_async_remote_copy(
            src_ref=zsnd.at[g], dst_ref=zrcv.at[g], send_sem=gz_send.at[g],
            recv_sem=gz_recv.at[g], device_id=at.before, device_id_type=MESH)

    for g in range(groups):
        for i in range(2):
            xsnd[g, i] = grads[g, i, T : 2 * T].astype(jnp.bfloat16)
    at.wait()
    for g in range(groups):
        grad_x(g).start()

    @pl.when(jnp.logical_not(at.odd))
    def _():
        for g in range(groups):
            for i in range(2):
                zsnd[g, i] = grads[g, i, 2 * T :].astype(jnp.bfloat16)
            grad_z(g).start()

    def pass_back(g):
        grad_x(g).wait_recv()
        for i in range(2):
            zsnd[g, i] = (
                grads[g, i, 2 * T :] + xrcv[g, i].astype(jnp.float32)).astype(jnp.bfloat16)
        grad_z(g).start()

    def row_results(n, w_ref, t):
        both = dot(w_ref[t], fan_out[n // per_group])
        for i in range(HEADS):
            lanes = pl.ds(pl.multiple_of(n * R + i * D, D), D)
            rows = slice(i * T, (i + 1) * T)
            o_vm[:, lanes] = both[rows, :D].astype(jnp.bfloat16)
            gq_vm[:, lanes] = (both[rows, D:] * scale).astype(jnp.bfloat16)

    def rest(t, carry):
        row_results(2 * t, w_0, t)
        row_results(2 * t + 1, w_1, t)

        @pl.when(jnp.logical_and(at.odd, jnp.logical_and(t >= 2, t < 2 + groups)))
        def _():
            pass_back(t - 2)

        return carry

    lax.fori_loop(0, stages // 2, rest, 0)

    @pl.when(jnp.logical_not(at.odd))
    def _():
        for g in range(groups):
            grad_x(g).wait_recv()

    for g in range(groups):
        grad_z(g).wait_recv()
        for i, out in enumerate((gk_vm, gv_vm)):
            mine = grads[g, i, :T] + zrcv[g, i].astype(jnp.float32)
            more = jnp.where(at.odd, 0.0, xrcv[g, i].astype(jnp.float32))
            out[:, g * D : (g + 1) * D] = (mine + more).astype(jnp.bfloat16)
    for g in range(groups):
        grad_x(g).wait_send()
        grad_z(g).wait_send()


def write_out(*refs):
    count = len(refs) // 2
    sems = refs[-1]
    copies = [pltpu.make_async_copy(refs[i], refs[count + i], sems.at[i]) for i in range(count)]
    for copy in copies:
        copy.start()
    for copy in copies:
        copy.wait()


def shards(mesh_shape, query, key_proj, value_projection, upstream, doc_start):
    groups = key_proj.shape[1] // D
    heads = query.shape[1] // D // groups
    stages = groups * heads // HEADS
    bf16, f32 = jnp.bfloat16, jnp.float32
    dma = pltpu.SemaphoreType.DMA
    vm = pltpu.VMEM
    in_hbm = pl.BlockSpec(memory_space=pltpu.HBM)
    in_vmem = pl.BlockSpec(memory_space=pltpu.VMEM)
    mib = 1024 * 1024
    shapes = (query.shape, query.shape, key_proj.shape, key_proj.shape)
    wide = vm((groups, T, heads * D), bf16)
    turned = vm((stages, D, R), bf16)
    weights = vm((stages // 2, R, 2 * S), bf16)
    block = vm((groups, 2, T, D), bf16)

    def held(*arrays):
        return [pltpu.with_memory_space_constraint(x, pltpu.VMEM) for x in arrays]

    q, up, q_t, up_t, fan_in, fan_out, tri, bias = pl.pallas_call(
        functools.partial(gather, mesh_shape, groups, heads),
        out_shape=(
            wide, wide, turned, turned,
            vm((groups, 2 * D, 2 * S), bf16), vm((groups, 2 * S, 2 * D), bf16),
            vm((T, T), bf16), vm((T, 2 * T), f32)),
        in_specs=[in_hbm] * 5,
        out_specs=(in_vmem,) * 8,
        scratch_shapes=[
            vm((groups, 2, S, D), bf16), vm(doc_start.shape, jnp.int32),
            dma((groups, 2)), dma((groups, 2)), dma] + [dma((groups,))] * 4,
        compiler_params=pltpu.CompilerParams(
            collective_id=0, has_side_effects=True, vmem_limit_bytes=8 * mib),
    )(*[
        pltpu.with_memory_space_constraint(x, pltpu.HBM)
        for x in (key_proj, value_projection, query, upstream, doc_start)
    ])
    w_0, w_1, grads = pl.pallas_call(
        functools.partial(attend, groups, heads),
        out_shape=(weights, weights, vm((groups, 2, S, D), f32)),
        in_specs=[in_vmem] * 7,
        out_specs=(in_vmem,) * 3,
        scratch_shapes=[vm((R, 2 * S), f32), vm((R, 2 * S), f32), vm((2, D, S), f32)],
        compiler_params=pltpu.CompilerParams(vmem_limit_bytes=16 * mib),
        cost_estimate=pl.CostEstimate(
            flops=8 * query.size * S, bytes_accessed=8 * query.size,
            transcendentals=query.size * 2),
    )(*held(q, up, q_t, up_t, fan_in, tri, bias))
    results = pl.pallas_call(
        functools.partial(scatter, mesh_shape, groups, heads),
        out_shape=tuple(vm(shape, bf16) for shape in shapes),
        in_specs=[in_vmem] * 4,
        out_specs=(in_vmem,) * 4,
        scratch_shapes=[block] * 4 + [dma((groups,))] * 4,
        compiler_params=pltpu.CompilerParams(
            collective_id=1, has_side_effects=True, vmem_limit_bytes=12 * mib),
    )(*held(grads, w_0, w_1, fan_out))
    return pl.pallas_call(
        write_out,
        out_shape=tuple(pltpu.HBM(shape, bf16) for shape in shapes),
        in_specs=[in_vmem] * 4,
        out_specs=(in_hbm,) * 4,
        scratch_shapes=[dma((4,))],
        compiler_params=pltpu.CompilerParams(vmem_limit_bytes=8 * mib),
    )(*held(*results))


def solution(mesh):
    mesh_shape = (mesh.shape["inner"], mesh.shape["outer"])
    rows = P(("uly", "inner", "outer"), None)
    return jax.shard_map(
        functools.partial(shards, mesh_shape), mesh=mesh,
        in_specs=(rows, rows, rows, rows, P(None, ("inner", "outer"))),
        out_specs=(rows, rows, rows, rows), check_vma=False)
```

```python
import functools
import math

import jax
import jax.numpy as jnp
from jax import lax
from jax.experimental import pallas as pl
from jax.experimental.pallas import tpu as pltpu
from jax.sharding import PartitionSpec as P

MESH = pl.DeviceIdType.MESH
D = 128
T = 128
HEADS = 4
R = HEADS * T
S = 3 * T
ROWS = 128
MASKED = -1e30

NN = (((1,), (0,)), ((), ()))


def dot(a, b):
    return lax.dot_general(a, b, NN, preferred_element_type=jnp.float32)


class Place:
    def __init__(self, mesh_shape):
        n_inner, n_outer = mesh_shape
        blocks = n_inner * n_outer
        self.chunks = 4 * blocks
        self.u = u = lax.axis_index("uly")
        b = lax.axis_index("inner") * n_outer + lax.axis_index("outer")
        late = u // 2
        self.half = u - 2 * late
        span = b + late * (2 * blocks - 1 - 2 * b)
        self.chunk = 2 * span + self.half
        self.odd = self.half == 1

        def device_of(c):
            at = c // 2
            is_late = at // blocks
            blk = at + is_late * (2 * blocks - 1 - 2 * at)
            return (c - 2 * at + 2 * is_late, blk // n_outer, blk % n_outer)

        self.partner = (u + 1 - 2 * self.half, lax.axis_index("inner"), lax.axis_index("outer"))
        self.after = device_of((self.chunk + 2) % self.chunks)
        self.before = device_of((self.chunk + self.chunks - 2) % self.chunks)

    def greet(self):
        barrier = pltpu.get_barrier_semaphore()
        for peer in (self.partner, self.after, self.before):
            pl.semaphore_signal(barrier, inc=1, device_id=peer, device_id_type=MESH)

    def wait(self):
        pl.semaphore_wait(pltpu.get_barrier_semaphore(), 3)


def gather(
    mesh_shape, groups, heads, k_hbm, v_hbm, q_hbm, up_hbm, st_hbm,
    q_vm, up_vm, q_t, up_t, fan_in, fan_out, tri, bias,
    kv, st_vm, own_sem, load_sem, st_sem, prev_send, prev_recv, old_send, old_recv,
):
    at = Place(mesh_shape)
    width = heads * D
    per_group = heads // HEADS
    at.greet()
    own = [
        pltpu.make_async_copy(
            src.at[:, pl.ds(g * D, D)], kv.at[g, i, pl.ds(0, T)], own_sem.at[g, i])
        for g in range(groups) for i, src in enumerate((k_hbm, v_hbm))
    ]
    starts = pltpu.make_async_copy(st_hbm, st_vm, st_sem)
    loads = [
        [
            pltpu.make_async_copy(
                src.at[:, pl.ds(g * width, width)], dst.at[g], load_sem.at[g, i])
            for i, (src, dst) in enumerate(((q_hbm, q_vm), (up_hbm, up_vm)))
        ]
        for g in range(groups)
    ]
    for copy in own + [starts] + sum(loads, []):
        copy.start()

    def send_old(g):
        return pltpu.make_async_remote_copy(
            src_ref=kv.at[g, :, pl.ds(0, T)], dst_ref=kv.at[g, :, pl.ds(2 * T, T)],
            send_sem=old_send.at[g], recv_sem=old_recv.at[g],
            device_id=at.after, device_id_type=MESH)

    def send_prev(g):
        return pltpu.make_async_remote_copy(
            src_ref=kv.at[g, :, pl.ds(pl.multiple_of(at.half * (2 * T), T), T)],
            dst_ref=kv.at[g, :, pl.ds(T, T)],
            send_sem=prev_send.at[g], recv_sem=prev_recv.at[g],
            device_id=at.partner, device_id_type=MESH)

    for copy in own:
        copy.wait()
    at.wait()
    for g in range(groups):
        send_old(g).start()

    @pl.when(jnp.logical_not(at.odd))
    def _():
        for g in range(groups):
            send_prev(g).start()

    starts.wait()
    u, chunk = at.u, at.chunk
    first = st_vm[0:1, :]
    for i in range(1, 4):
        first = jnp.where(u == i, st_vm[i : i + 1, :], first)
    first = first - chunk * T
    key_at = lax.broadcasted_iota(jnp.int32, (T, T), 0)
    query_at = lax.broadcasted_iota(jnp.int32, (T, T), 1)
    seen = (
        (key_at <= query_at) & (key_at >= first),
        key_at - T >= first,
        (key_at > query_at) & (key_at - 2 * T >= first),
    )
    near = jnp.where(seen[0] | seen[2], 0.0, MASKED)
    bias[:, :T] = near.T
    bias[:, T:] = jnp.where(seen[1], 0.0, MASKED).T
    tri[...] = jnp.where(key_at >= query_at, 1.0, 0.0).astype(jnp.bfloat16)
    fan_in[...] = jnp.zeros_like(fan_in)
    fan_out[...] = jnp.zeros_like(fan_out)

    def spread(g, lo, hi):
        fan_in[g, :D, lo:hi] = kv[g, 0, lo:hi].T
        fan_in[g, D:, S + lo : S + hi] = kv[g, 1, lo:hi].T
        fan_out[g, lo:hi, :D] = kv[g, 1, lo:hi]
        fan_out[g, S + lo : S + hi, D:] = kv[g, 0, lo:hi]

    for g in range(groups):
        spread(g, 0, T)

    def lanes_of(n):
        at = (n % per_group) * R
        return [pl.ds(pl.multiple_of(at + i * D, D), D) for i in range(HEADS)]

    def rows_of(ref, n):
        return jnp.concatenate([ref[n // per_group, :, c] for c in lanes_of(n)], axis=0)

    def turn(n, carry):
        q_t[n] = rows_of(q_vm, n).T
        up_t[n] = rows_of(up_vm, n).T
        return carry

    for g in range(groups):
        for copy in loads[g]:
            copy.wait()
        lax.fori_loop(g * per_group, (g + 1) * per_group, turn, 0)

    @pl.when(at.odd)
    def _():
        for g in range(groups):
            send_old(g).wait_recv()
            send_prev(g).start()

    @pl.when(jnp.logical_not(at.odd))
    def _():
        for g in range(groups):
            send_old(g).wait_recv()

    for g in range(groups):
        spread(g, 2 * T, S)
    for g in range(groups):
        send_prev(g).wait_recv()
        spread(g, T, 2 * T)
    for g in range(groups):
        send_prev(g).wait_send()
        send_old(g).wait_send()


def attend(
    mesh_shape, groups, heads,
    q_vm, up_vm, q_t, up_t, fan_in, fan_out, tri, bias,
    o_vm, gq_vm, gk_vm, gv_vm,
    s_0, s_1, w_0, w_1, acc, own, old, xsnd, xrcv, zsnd, zrcv,
    gx_send, gx_recv, gz_send, gz_recv,
):
    at = Place(mesh_shape)
    per_group = heads // HEADS
    stages = groups * per_group
    steps = per_group // 2
    scale = D ** -0.5
    rate = scale * math.log2(math.e)
    at.greet()

    def grad_x(g):
        return pltpu.make_async_remote_copy(
            src_ref=xsnd.at[g], dst_ref=xrcv.at[g], send_sem=gx_send.at[g],
            recv_sem=gx_recv.at[g], device_id=at.partner, device_id_type=MESH)

    def grad_z(g):
        return pltpu.make_async_remote_copy(
            src_ref=zsnd.at[g], dst_ref=zrcv.at[g], send_sem=gz_send.at[g],
            recv_sem=gz_recv.at[g], device_id=at.before, device_id_type=MESH)

    def lanes_of(n):
        at = (n % per_group) * R
        return [pl.ds(pl.multiple_of(at + i * D, D), D) for i in range(HEADS)]

    def rows_of(ref, n):
        return jnp.concatenate([ref[n // per_group, :, c] for c in lanes_of(n)], axis=0)

    def scores(n, s_out):
        n = jnp.minimum(n, stages - 1)
        both = jnp.concatenate([rows_of(q_vm, n), rows_of(up_vm, n)], axis=1)
        s_out[...] = dot(both, fan_in[n // per_group])

    def soften(s_ref, w_out, t):
        for at in range(0, R, ROWS):
            rows = slice(at, at + ROWS)
            own_k, mid_k, old_k = [slice(i * T, (i + 1) * T) for i in range(3)]
            own_v, mid_v, old_v = [slice(i * T, (i + 1) * T) for i in range(3, 6)]
            here = slice(at % T, at % T + ROWS)
            key_at = lax.broadcasted_iota(jnp.int32, (ROWS, T), 1)
            query_at = lax.broadcasted_iota(jnp.int32, (ROWS, T), 0) + at % T
            lower = key_at <= query_at
            s_mix = jnp.where(lower, s_ref[rows, own_k], s_ref[rows, old_k]) + bias[here, :T]
            s_mid = s_ref[rows, mid_k] + bias[here, T:]
            top = jnp.max(jnp.maximum(s_mix, s_mid), axis=1, keepdims=True)
            e_mix = jnp.exp2((s_mix - top) * rate)
            e_mid = jnp.exp2((s_mid - top) * rate)
            inverse = 1.0 / jnp.sum(e_mix + e_mid, axis=1, keepdims=True)
            dp_mix = jnp.where(lower, s_ref[rows, own_v], s_ref[rows, old_v])
            dp_mid = s_ref[rows, mid_v]
            w_mix = e_mix * inverse
            w_mid = e_mid * inverse
            delta = jnp.sum(w_mix * dp_mix + w_mid * dp_mid, axis=1, keepdims=True)
            ds_mix = w_mix * (dp_mix - delta)
            ds_mid = w_mid * (dp_mid - delta)
            for mix, mid, base in ((w_mix, w_mid, 0), (ds_mix, ds_mid, S)):
                mix = mix.astype(jnp.bfloat16)
                own_part = mix * tri[here, :]
                w_out[t, rows, base : base + T] = own_part
                w_out[t, rows, base + T : base + 2 * T] = mid.astype(jnp.bfloat16)
                w_out[t, rows, base + 2 * T : base + S] = mix - own_part

    def key_results(n, w_ref, t):
        n = jnp.maximum(n, 0)
        t = jnp.maximum(t, 0)
        acc[1] += dot(up_t[n], w_ref[t, :, :S])
        acc[0] += dot(q_t[n], w_ref[t, :, S:])

    def row_results(n, w_ref, t):
        both = dot(w_ref[t], fan_out[n // per_group])
        for i in range(HEADS):
            lanes = pl.ds(pl.multiple_of(n * R + i * D, D), D)
            rows = slice(i * T, (i + 1) * T)
            o_vm[:, lanes] = both[rows, :D].astype(jnp.bfloat16)
            gq_vm[:, lanes] = (both[rows, D:] * scale).astype(jnp.bfloat16)

    def finish_group(g):
        for i in range(2):
            grad = acc[i] * scale if i == 0 else acc[i]
            own[g, i] = grad[:, :T].T
            xsnd[g, i] = grad[:, T : 2 * T].T.astype(jnp.bfloat16)
            old[g, i] = grad[:, 2 * T :].T
        acc[...] = jnp.zeros_like(acc)
        grad_x(g).start()

        @pl.when(jnp.logical_not(at.odd))
        def _():
            zsnd[g] = old[g].astype(jnp.bfloat16)
            grad_z(g).start()

    def pass_back(g):
        @pl.when(at.odd)
        def _():
            grad_x(g).wait_recv()
            zsnd[g] = (old[g] + xrcv[g].astype(jnp.float32)).astype(jnp.bfloat16)
            grad_z(g).start()

    acc[...] = jnp.zeros_like(acc)
    w_1[0] = jnp.zeros(w_1.shape[1:], w_1.dtype)
    scores(0, s_0)

    def step(t, carry):
        g = t // steps
        i = t % steps
        n = 2 * t

        @pl.when(t == steps)
        def _():
            at.wait()

        @pl.when(jnp.logical_and(i == steps - 1, g > 0))
        def _():
            pass_back(g - 1)

        scores(n + 1, s_1)
        soften(s_0, w_0, t)
        key_results(n - 1, w_1, t - 1)

        @pl.when(jnp.logical_and(i == 0, g > 0))
        def _():
            finish_group(g - 1)

        scores(n + 2, s_0)
        soften(s_1, w_1, t)
        key_results(n, w_0, t)
        return carry

    lax.fori_loop(0, groups * steps, step, 0)
    key_results(stages - 1, w_1, stages // 2 - 1)
    finish_group(groups - 1)

    def rest(t, carry):
        row_results(2 * t, w_0, t)
        row_results(2 * t + 1, w_1, t)

        @pl.when(t == 2)
        def _():
            pass_back(groups - 1)

        return carry

    lax.fori_loop(0, stages // 2, rest, 0)

    for g in range(groups):
        @pl.when(jnp.logical_not(at.odd))
        def _():
            grad_x(g).wait_recv()
            own[g] += xrcv[g].astype(jnp.float32)

        grad_z(g).wait_recv()
        for i, out in enumerate((gk_vm, gv_vm)):
            out[:, g * D : (g + 1) * D] = (
                own[g, i] + zrcv[g, i].astype(jnp.float32)).astype(jnp.bfloat16)
    for g in range(groups):
        for copy in (grad_x(g), grad_z(g)):
            copy.wait_send()


def write_out(*refs):
    count = len(refs) // 2
    sems = refs[-1]
    copies = [pltpu.make_async_copy(refs[i], refs[count + i], sems.at[i]) for i in range(count)]
    for copy in copies:
        copy.start()
    for copy in copies:
        copy.wait()


def shards(mesh_shape, query, key_proj, value_projection, upstream, doc_start):
    groups = key_proj.shape[1] // D
    heads = query.shape[1] // D // groups
    stages = groups * heads // HEADS
    bf16, f32 = jnp.bfloat16, jnp.float32
    dma = pltpu.SemaphoreType.DMA
    vm = pltpu.VMEM
    in_hbm = pl.BlockSpec(memory_space=pltpu.HBM)
    in_vmem = pl.BlockSpec(memory_space=pltpu.VMEM)
    mib = 1024 * 1024
    shapes = (query.shape, query.shape, key_proj.shape, key_proj.shape)
    wide = vm((groups, T, heads * D), bf16)
    turned = vm((stages, D, R), bf16)
    weights = vm((stages // 2, R, 2 * S), bf16)
    block = vm((groups, 2, T, D), bf16)

    def held(*arrays):
        return [pltpu.with_memory_space_constraint(x, pltpu.VMEM) for x in arrays]

    q, up, q_t, up_t, fan_in, fan_out, tri, bias = pl.pallas_call(
        functools.partial(gather, mesh_shape, groups, heads),
        out_shape=(
            wide, wide, turned, turned,
            vm((groups, 2 * D, 2 * S), bf16), vm((groups, 2 * S, 2 * D), bf16),
            vm((T, T), bf16), vm((T, 2 * T), f32)),
        in_specs=[in_hbm] * 5,
        out_specs=(in_vmem,) * 8,
        scratch_shapes=[
            vm((groups, 2, S, D), bf16), vm(doc_start.shape, jnp.int32),
            dma((groups, 2)), dma((groups, 2)), dma] + [dma((groups,))] * 4,
        compiler_params=pltpu.CompilerParams(
            collective_id=0, has_side_effects=True, vmem_limit_bytes=8 * mib),
    )(*[
        pltpu.with_memory_space_constraint(x, pltpu.HBM)
        for x in (key_proj, value_projection, query, upstream, doc_start)
    ])
    results = pl.pallas_call(
        functools.partial(attend, mesh_shape, groups, heads),
        out_shape=tuple(vm(shape, bf16) for shape in shapes),
        in_specs=[in_vmem] * 8,
        out_specs=(in_vmem,) * 4,
        scratch_shapes=[
            vm((R, 2 * S), f32), vm((R, 2 * S), f32), weights, weights, vm((2, D, S), f32),
            vm((groups, 2, T, D), f32), vm((groups, 2, T, D), f32),
            block, block, block, block] + [dma((groups,))] * 4,
        compiler_params=pltpu.CompilerParams(
            collective_id=1, has_side_effects=True, vmem_limit_bytes=28 * mib),
        cost_estimate=pl.CostEstimate(
            flops=12 * query.size * S, bytes_accessed=8 * query.size,
            transcendentals=query.size * 2),
    )(*held(q, up, q_t, up_t, fan_in, fan_out, tri, bias))
    return pl.pallas_call(
        write_out,
        out_shape=tuple(pltpu.HBM(shape, bf16) for shape in shapes),
        in_specs=[in_vmem] * 4,
        out_specs=(in_hbm,) * 4,
        scratch_shapes=[dma((4,))],
        compiler_params=pltpu.CompilerParams(vmem_limit_bytes=8 * mib),
    )(*held(*results))


def solution(mesh):
    mesh_shape = (mesh.shape["inner"], mesh.shape["outer"])
    rows = P(("uly", "inner", "outer"), None)
    return jax.shard_map(
        functools.partial(shards, mesh_shape), mesh=mesh,
        in_specs=(rows, rows, rows, rows, P(None, ("inner", "outer"))),
        out_specs=(rows, rows, rows, rows), check_vma=False)
```

```python
import functools
import math

import jax
import jax.numpy as jnp
from jax import lax
from jax.experimental import pallas as pl
from jax.experimental.pallas import tpu as pltpu
from jax.sharding import PartitionSpec as P

MESH = pl.DeviceIdType.MESH
D = 128
T = 128
HEADS = 4
R = HEADS * T
S = 3 * T
ROWS = 128
MASKED = -1e30

NN = (((1,), (0,)), ((), ()))


def dot(a, b):
    return lax.dot_general(a, b, NN, preferred_element_type=jnp.float32)


class Place:
    def __init__(self, mesh_shape):
        n_inner, n_outer = mesh_shape
        blocks = n_inner * n_outer
        self.chunks = 4 * blocks
        self.u = u = lax.axis_index("uly")
        b = lax.axis_index("inner") * n_outer + lax.axis_index("outer")
        late = u // 2
        self.half = u - 2 * late
        span = b + late * (2 * blocks - 1 - 2 * b)
        self.chunk = 2 * span + self.half
        self.odd = self.half == 1

        def device_of(c):
            at = c // 2
            is_late = at // blocks
            blk = at + is_late * (2 * blocks - 1 - 2 * at)
            return (c - 2 * at + 2 * is_late, blk // n_outer, blk % n_outer)

        self.partner = (u + 1 - 2 * self.half, lax.axis_index("inner"), lax.axis_index("outer"))
        self.after = device_of((self.chunk + 2) % self.chunks)
        self.before = device_of((self.chunk + self.chunks - 2) % self.chunks)

    def greet(self):
        barrier = pltpu.get_barrier_semaphore()
        for peer in (self.partner, self.after, self.before):
            pl.semaphore_signal(barrier, inc=1, device_id=peer, device_id_type=MESH)

    def wait(self):
        pl.semaphore_wait(pltpu.get_barrier_semaphore(), 3)


def gather(
    mesh_shape, groups, heads, k_hbm, v_hbm, q_hbm, up_hbm, st_hbm,
    q_vm, up_vm, q_t, up_t, fan_in, fan_out, tri, bias,
    kv, st_vm, own_sem, load_sem, st_sem, prev_send, prev_recv, old_send, old_recv,
):
    at = Place(mesh_shape)
    width = heads * D
    per_group = heads // HEADS
    at.greet()
    own = [
        pltpu.make_async_copy(
            src.at[:, pl.ds(g * D, D)], kv.at[g, i, pl.ds(0, T)], own_sem.at[g, i])
        for g in range(groups) for i, src in enumerate((k_hbm, v_hbm))
    ]
    starts = pltpu.make_async_copy(st_hbm, st_vm, st_sem)
    loads = [
        [
            pltpu.make_async_copy(
                src.at[:, pl.ds(g * width, width)], dst.at[g], load_sem.at[g, i])
            for i, (src, dst) in enumerate(((q_hbm, q_vm), (up_hbm, up_vm)))
        ]
        for g in range(groups)
    ]
    for copy in own + [starts] + sum(loads, []):
        copy.start()

    def send_old(g):
        return pltpu.make_async_remote_copy(
            src_ref=kv.at[g, :, pl.ds(0, T)], dst_ref=kv.at[g, :, pl.ds(2 * T, T)],
            send_sem=old_send.at[g], recv_sem=old_recv.at[g],
            device_id=at.after, device_id_type=MESH)

    def send_prev(g):
        return pltpu.make_async_remote_copy(
            src_ref=kv.at[g, :, pl.ds(pl.multiple_of(at.half * (2 * T), T), T)],
            dst_ref=kv.at[g, :, pl.ds(T, T)],
            send_sem=prev_send.at[g], recv_sem=prev_recv.at[g],
            device_id=at.partner, device_id_type=MESH)

    for copy in own:
        copy.wait()
    at.wait()
    for g in range(groups):
        send_old(g).start()

    @pl.when(jnp.logical_not(at.odd))
    def _():
        for g in range(groups):
            send_prev(g).start()

    starts.wait()
    u, chunk = at.u, at.chunk
    first = st_vm[0:1, :]
    for i in range(1, 4):
        first = jnp.where(u == i, st_vm[i : i + 1, :], first)
    first = first - chunk * T
    key_at = lax.broadcasted_iota(jnp.int32, (T, T), 0)
    query_at = lax.broadcasted_iota(jnp.int32, (T, T), 1)
    seen = (
        (key_at <= query_at) & (key_at >= first),
        key_at - T >= first,
        (key_at > query_at) & (key_at - 2 * T >= first),
    )
    near = jnp.where(seen[0] | seen[2], 0.0, MASKED)
    bias[:, :T] = near.T
    bias[:, T:] = jnp.where(seen[1], 0.0, MASKED).T
    tri[...] = jnp.where(key_at >= query_at, 1.0, 0.0).astype(jnp.bfloat16)
    fan_in[...] = jnp.zeros_like(fan_in)
    fan_out[...] = jnp.zeros_like(fan_out)

    def spread(g, lo, hi):
        fan_in[g, :D, lo:hi] = kv[g, 0, lo:hi].T
        fan_in[g, D:, S + lo : S + hi] = kv[g, 1, lo:hi].T
        fan_out[g, lo:hi, :D] = kv[g, 1, lo:hi]
        fan_out[g, S + lo : S + hi, D:] = kv[g, 0, lo:hi]

    for g in range(groups):
        spread(g, 0, T)

    def lanes_of(n):
        at = (n % per_group) * R
        return [pl.ds(pl.multiple_of(at + i * D, D), D) for i in range(HEADS)]

    def rows_of(ref, n):
        return jnp.concatenate([ref[n // per_group, :, c] for c in lanes_of(n)], axis=0)

    def turn(n, carry):
        q_t[n] = rows_of(q_vm, n).T
        up_t[n] = rows_of(up_vm, n).T
        return carry

    for g in range(groups):
        for copy in loads[g]:
            copy.wait()
        lax.fori_loop(g * per_group, (g + 1) * per_group, turn, 0)

    @pl.when(at.odd)
    def _():
        for g in range(groups):
            send_old(g).wait_recv()
            send_prev(g).start()

    @pl.when(jnp.logical_not(at.odd))
    def _():
        for g in range(groups):
            send_old(g).wait_recv()

    for g in range(groups):
        spread(g, 2 * T, S)
    for g in range(groups):
        send_prev(g).wait_recv()
        spread(g, T, 2 * T)
    for g in range(groups):
        send_prev(g).wait_send()
        send_old(g).wait_send()


def attend(
    mesh_shape, groups, heads,
    q_vm, up_vm, q_t, up_t, fan_in, fan_out, tri, bias,
    o_vm, gq_vm, gk_vm, gv_vm,
    s_0, s_1, w_0, w_1, acc, own, old, xsnd, xrcv, zsnd, zrcv,
    gx_send, gx_recv, gz_send, gz_recv,
):
    at = Place(mesh_shape)
    per_group = heads // HEADS
    stages = groups * per_group
    steps = per_group // 2
    scale = D ** -0.5
    rate = scale * math.log2(math.e)
    at.greet()

    def grad_x(g):
        return pltpu.make_async_remote_copy(
            src_ref=xsnd.at[g], dst_ref=xrcv.at[g], send_sem=gx_send.at[g],
            recv_sem=gx_recv.at[g], device_id=at.partner, device_id_type=MESH)

    def grad_z(g):
        return pltpu.make_async_remote_copy(
            src_ref=zsnd.at[g], dst_ref=zrcv.at[g], send_sem=gz_send.at[g],
            recv_sem=gz_recv.at[g], device_id=at.before, device_id_type=MESH)

    def lanes_of(n):
        at = (n % per_group) * R
        return [pl.ds(pl.multiple_of(at + i * D, D), D) for i in range(HEADS)]

    def rows_of(ref, n):
        return jnp.concatenate([ref[n // per_group, :, c] for c in lanes_of(n)], axis=0)

    def scores(n, s_out):
        n = jnp.minimum(n, stages - 1)
        both = jnp.concatenate([rows_of(q_vm, n), rows_of(up_vm, n)], axis=1)
        s_out[...] = dot(both, fan_in[n // per_group])

    def soften(s_ref, w_out, t):
        for at in range(0, R, ROWS):
            rows = slice(at, at + ROWS)
            own_k, mid_k, old_k = [slice(i * T, (i + 1) * T) for i in range(3)]
            own_v, mid_v, old_v = [slice(i * T, (i + 1) * T) for i in range(3, 6)]
            here = slice(at % T, at % T + ROWS)
            key_at = lax.broadcasted_iota(jnp.int32, (ROWS, T), 1)
            query_at = lax.broadcasted_iota(jnp.int32, (ROWS, T), 0) + at % T
            lower = key_at <= query_at
            s_mix = jnp.where(lower, s_ref[rows, own_k], s_ref[rows, old_k]) + bias[here, :T]
            s_mid = s_ref[rows, mid_k] + bias[here, T:]
            top = jnp.max(jnp.maximum(s_mix, s_mid), axis=1, keepdims=True)
            e_mix = jnp.exp2((s_mix - top) * rate)
            e_mid = jnp.exp2((s_mid - top) * rate)
            inverse = 1.0 / jnp.sum(e_mix + e_mid, axis=1, keepdims=True)
            dp_mix = jnp.where(lower, s_ref[rows, own_v], s_ref[rows, old_v])
            dp_mid = s_ref[rows, mid_v]
            w_mix = e_mix * inverse
            w_mid = e_mid * inverse
            delta = jnp.sum(w_mix * dp_mix + w_mid * dp_mid, axis=1, keepdims=True)
            ds_mix = w_mix * (dp_mix - delta)
            ds_mid = w_mid * (dp_mid - delta)
            for mix, mid, base in ((w_mix, w_mid, 0), (ds_mix, ds_mid, S)):
                mix = mix.astype(jnp.bfloat16)
                own_part = mix * tri[here, :]
                w_out[t, rows, base : base + T] = own_part
                w_out[t, rows, base + T : base + 2 * T] = mid.astype(jnp.bfloat16)
                w_out[t, rows, base + 2 * T : base + S] = mix - own_part

    def key_results(n, w_ref, t):
        n = jnp.maximum(n, 0)
        t = jnp.maximum(t, 0)
        acc[1] += dot(up_t[n], w_ref[t, :, :S])
        acc[0] += dot(q_t[n], w_ref[t, :, S:])

    def row_results(n, w_ref, t):
        both = dot(w_ref[t], fan_out[n // per_group])
        for i in range(HEADS):
            lanes = pl.ds(pl.multiple_of(n * R + i * D, D), D)
            rows = slice(i * T, (i + 1) * T)
            o_vm[:, lanes] = both[rows, :D].astype(jnp.bfloat16)
            gq_vm[:, lanes] = (both[rows, D:] * scale).astype(jnp.bfloat16)

    def finish_group(g):
        for i in range(2):
            grad = acc[i] * scale if i == 0 else acc[i]
            own[g, i] = grad[:, :T].T
            xsnd[g, i] = grad[:, T : 2 * T].T.astype(jnp.bfloat16)
            old[g, i] = grad[:, 2 * T :].T
        acc[...] = jnp.zeros_like(acc)
        grad_x(g).start()

        @pl.when(jnp.logical_not(at.odd))
        def _():
            zsnd[g] = old[g].astype(jnp.bfloat16)
            grad_z(g).start()

    def pass_back(g):
        @pl.when(at.odd)
        def _():
            grad_x(g).wait_recv()
            zsnd[g] = (old[g] + xrcv[g].astype(jnp.float32)).astype(jnp.bfloat16)
            grad_z(g).start()

    acc[...] = jnp.zeros_like(acc)
    w_1[0] = jnp.zeros(w_1.shape[1:], w_1.dtype)
    scores(0, s_0)

    def step(t, carry):
        g = t // steps
        i = t % steps
        n = 2 * t

        @pl.when(t == steps)
        def _():
            at.wait()

        scores(n + 1, s_1)
        soften(s_0, w_0, t)
        key_results(n - 1, w_1, t - 1)

        @pl.when(jnp.logical_and(i == 0, g > 0))
        def _():
            finish_group(g - 1)

        scores(n + 2, s_0)
        soften(s_1, w_1, t)
        key_results(n, w_0, t)

        @pl.when(jnp.logical_and(i == steps - 1, g > 0))
        def _():
            pass_back(g - 1)

        return carry

    lax.fori_loop(0, groups * steps, step, 0)
    key_results(stages - 1, w_1, stages // 2 - 1)
    finish_group(groups - 1)

    def rest(t, carry):
        row_results(2 * t, w_0, t)
        row_results(2 * t + 1, w_1, t)

        @pl.when(t == 2)
        def _():
            pass_back(groups - 1)

        return carry

    lax.fori_loop(0, stages // 2, rest, 0)

    for g in range(groups):
        @pl.when(jnp.logical_not(at.odd))
        def _():
            grad_x(g).wait_recv()
            own[g] += xrcv[g].astype(jnp.float32)

        grad_z(g).wait_recv()
        for i, out in enumerate((gk_vm, gv_vm)):
            out[:, g * D : (g + 1) * D] = (
                own[g, i] + zrcv[g, i].astype(jnp.float32)).astype(jnp.bfloat16)
    for g in range(groups):
        for copy in (grad_x(g), grad_z(g)):
            copy.wait_send()


def write_out(*refs):
    count = len(refs) // 2
    sems = refs[-1]
    copies = [pltpu.make_async_copy(refs[i], refs[count + i], sems.at[i]) for i in range(count)]
    for copy in copies:
        copy.start()
    for copy in copies:
        copy.wait()


def shards(mesh_shape, query, key_proj, value_projection, upstream, doc_start):
    groups = key_proj.shape[1] // D
    heads = query.shape[1] // D // groups
    stages = groups * heads // HEADS
    bf16, f32 = jnp.bfloat16, jnp.float32
    dma = pltpu.SemaphoreType.DMA
    vm = pltpu.VMEM
    in_hbm = pl.BlockSpec(memory_space=pltpu.HBM)
    in_vmem = pl.BlockSpec(memory_space=pltpu.VMEM)
    mib = 1024 * 1024
    shapes = (query.shape, query.shape, key_proj.shape, key_proj.shape)
    wide = vm((groups, T, heads * D), bf16)
    turned = vm((stages, D, R), bf16)
    weights = vm((stages // 2, R, 2 * S), bf16)
    block = vm((groups, 2, T, D), bf16)

    def held(*arrays):
        return [pltpu.with_memory_space_constraint(x, pltpu.VMEM) for x in arrays]

    q, up, q_t, up_t, fan_in, fan_out, tri, bias = pl.pallas_call(
        functools.partial(gather, mesh_shape, groups, heads),
        out_shape=(
            wide, wide, turned, turned,
            vm((groups, 2 * D, 2 * S), bf16), vm((groups, 2 * S, 2 * D), bf16),
            vm((T, T), bf16), vm((T, 2 * T), f32)),
        in_specs=[in_hbm] * 5,
        out_specs=(in_vmem,) * 8,
        scratch_shapes=[
            vm((groups, 2, S, D), bf16), vm(doc_start.shape, jnp.int32),
            dma((groups, 2)), dma((groups, 2)), dma] + [dma((groups,))] * 4,
        compiler_params=pltpu.CompilerParams(
            collective_id=0, has_side_effects=True, vmem_limit_bytes=8 * mib),
    )(*[
        pltpu.with_memory_space_constraint(x, pltpu.HBM)
        for x in (key_proj, value_projection, query, upstream, doc_start)
    ])
    results = pl.pallas_call(
        functools.partial(attend, mesh_shape, groups, heads),
        out_shape=tuple(vm(shape, bf16) for shape in shapes),
        in_specs=[in_vmem] * 8,
        out_specs=(in_vmem,) * 4,
        scratch_shapes=[
            vm((R, 2 * S), f32), vm((R, 2 * S), f32), weights, weights, vm((2, D, S), f32),
            vm((groups, 2, T, D), f32), vm((groups, 2, T, D), f32),
            block, block, block, block] + [dma((groups,))] * 4,
        compiler_params=pltpu.CompilerParams(
            collective_id=1, has_side_effects=True, vmem_limit_bytes=28 * mib),
        cost_estimate=pl.CostEstimate(
            flops=12 * query.size * S, bytes_accessed=8 * query.size,
            transcendentals=query.size * 2),
    )(*held(q, up, q_t, up_t, fan_in, fan_out, tri, bias))
    return pl.pallas_call(
        write_out,
        out_shape=tuple(pltpu.HBM(shape, bf16) for shape in shapes),
        in_specs=[in_vmem] * 4,
        out_specs=(in_hbm,) * 4,
        scratch_shapes=[dma((4,))],
        compiler_params=pltpu.CompilerParams(vmem_limit_bytes=8 * mib),
    )(*held(*results))


def solution(mesh):
    mesh_shape = (mesh.shape["inner"], mesh.shape["outer"])
    rows = P(("uly", "inner", "outer"), None)
    return jax.shard_map(
        functools.partial(shards, mesh_shape), mesh=mesh,
        in_specs=(rows, rows, rows, rows, P(None, ("inner", "outer"))),
        out_specs=(rows, rows, rows, rows), check_vma=False)
```
